32 devices in a mesh: beam: 4 (over y, core), strip: 8 (over z, x).
Axes of the slice: x: 2, y: 2, z: 4, core: 2. Of those that a mesh axis runs over, the one named last changes fastest.
Arguments:
- atoms: int32 [2, 1536, 4096], P(None, 'strip'), may hold values from 0 to 3
- phases: float32 [2, 4], replicated, may hold values from 0.2 to 3
- aperture: float32 [8], P('beam'), may hold values from 0.3 to 3
- tilts: int32 [8, 2], P('beam'), may hold values from -16 to 16
- positions: int32 [256, 2], P('strip'), may hold values from 0 to 4095, as said below
Outputs:
- intensity: float32 [256, 16384], P('strip')
The draws below stay inside these ranges and needn't reach their ends.
Inputs may be any that keep to these rules, and one draw needn't show every extreme that they name: `positions`: probes 32 * s to 32 * s + 31 have their row in rows 192 * s to 192 * s + 191; columns lie in 0 to 4095. Probe 0 lies at row 0, column 0, and the last probe at row 1535, column 4095.
All inputs are finite; a program needn't handle non-finite values.
Results may differ from the reference program's by a relative error of at most 0.02.
Values may be sent and summed in bfloat16 or wider, within the bound.
No kernel may reach another device: no remote copies, remote signals or barrier semaphores. Data moves between devices by JAX's collectives and lax.ppermute only.
A program may use at most 192 MiB of HBM per device.

```python
import math
import jax
import jax.numpy as jnp
from jax import lax

NXG = 4096
HALFW = 32
SLICES = 2
TYPES = 4
TILT = 16
WIN = 128
ROWS_DEV = 192
PROBE_DEV = 32
NY = 1536
BEAMS = 8
PROBES = 256


def draw_positions(key, part):
    row_key, col_key = jax.random.split(key)
    owner_strip = jnp.arange(PROBES, dtype=jnp.int32) // PROBE_DEV
    row_offset = jax.random.randint(row_key, (PROBES,), 0, ROWS_DEV, dtype=jnp.int32)
    columns = jax.random.randint(col_key, (PROBES,), 0, NXG, dtype=jnp.int32)
    row_offset = row_offset.at[0].set(0).at[PROBES - 1].set(ROWS_DEV - 1)
    columns = columns.at[0].set(0).at[PROBES - 1].set(NXG - 1)
    return jnp.stack([owner_strip * ROWS_DEV + row_offset, columns], axis=1)


def set_ends(array, rng, least, high):
    index_at = [jax.random.randint(jax.random.fold_in(rng, axis), (), 0, length) for axis, length in enumerate(array.shape)]
    widest = array.shape.index(max(array.shape))
    beside = index_at[:widest] + [(index_at[widest] + 1) % array.shape[widest]] + index_at[widest + 1:]
    return array.at[tuple(index_at)].set(least).at[tuple(beside)].set(high)


def block_levels(own_key, shape, pieces, smallest, high):
    loudness = 1.0
    for dim, blocks in pieces:
        draws = jax.random.uniform(jax.random.fold_in(jax.random.fold_in(own_key, 6), dim), (blocks,), jnp.float32, smallest / len(pieces), high / len(pieces))
        loudness = loudness * jnp.repeat(jnp.exp(draws), shape[dim] // blocks).reshape((-1,) + (1,) * (len(shape) - 1 - dim))
    return loudness


def setup_inputs(seed: int = 0) -> dict:
    key_list = jax.random.split(jax.random.key(seed), 6)
    return {
        "atoms": set_ends(jax.random.randint(key_list[0], (SLICES, NY, NXG), 0, TYPES), jax.random.fold_in(key_list[0], 1), 0, TYPES - 1).astype(jnp.int32),
        "phases": jnp.clip(jax.random.uniform(key_list[1], (SLICES, TYPES), jnp.float32, 0.2, 3.0), 0.2, 3.0),
        "aperture": jnp.clip(jnp.exp(math.log(3.0) - 2.3025851 * jax.random.uniform(key_list[2], (BEAMS,), jnp.float32) ** block_levels(key_list[2], (BEAMS,), ((0, 4),), -0.2, 0.2)), 0.3, 3.0),
        "tilts": set_ends(jax.random.randint(key_list[3], (BEAMS, 2), 0 - TILT, TILT + 1), jax.random.fold_in(key_list[3], 1), 0 - TILT, TILT).astype(jnp.int32),
        "positions": draw_positions(jax.random.fold_in(key_list[5], 71), 0),
    }


def band_taps(offset):
    steps_all = jnp.arange(-HALFW, HALFW + 1).astype(jnp.float32)
    weights_all = 1.0 - 0.5 * (steps_all / (HALFW + 1.0)) ** 2
    norm_scale = jnp.sqrt(jnp.sum(weights_all * weights_all))
    weight = (1.0 - 0.5 * (offset / (HALFW + 1.0)) ** 2) / norm_scale
    chirp_phase = math.pi * offset * offset / (2.0 * HALFW + 1.0)
    inside = jnp.abs(offset) <= HALFW
    real_part = jnp.where(inside, jnp.cos(chirp_phase) * weight, 0.0)
    imag_part = jnp.where(inside, jnp.sin(chirp_phase) * weight, 0.0)
    return (real_part.astype(jnp.bfloat16), imag_part.astype(jnp.bfloat16))

def spectrum(length):
    position = jnp.arange(length)
    offset = jnp.where(position <= length // 2, position, position - length).astype(jnp.float32)
    real_part, imag_part = band_taps(offset)
    kernel = real_part.astype(jnp.float32) + 1j * imag_part.astype(jnp.float32)
    return jnp.fft.fft(kernel)

def convolve(real_in, imag_in, kernel_ft, axis_id):
    values_in = real_in.astype(jnp.float32) + 1j * imag_in.astype(jnp.float32)
    if axis_id == 0:
        spread = kernel_ft[:, None]
    else:
        spread = kernel_ft[None, :]
    result = jnp.fft.ifft(jnp.fft.fft(values_in, axis=axis_id) * spread, axis=axis_id)
    return (jnp.real(result).astype(jnp.float32), jnp.imag(result).astype(jnp.float32))

def slice_angles(atom_map, phase_row):
    angles = jnp.zeros(atom_map.shape, jnp.float32)
    for atom_type in range(TYPES):
        angles = angles + jnp.where(atom_map == atom_type, phase_row[atom_type], 0.0)
    return angles

def reference(atoms, phases, aperture, tilts, positions):
    rows_all = jnp.arange(NY, dtype=jnp.int32)
    cols_all = jnp.arange(NXG, dtype=jnp.int32)
    ft_cols = spectrum(NXG)
    ft_rows = spectrum(NY)
    trans_real = []
    trans_imag = []
    for layer in range(SLICES):
        angles = slice_angles(atoms[layer], phases[layer])
        trans_real.append(jnp.cos(angles))
        trans_imag.append(jnp.sin(angles))
    half_win = WIN // 2
    offsets = jnp.arange(WIN, dtype=jnp.int32) - half_win
    win_rows = (positions[:, 0][:, None] + offsets[None, :]) % NY
    win_cols = (positions[:, 1][:, None] + offsets[None, :]) % NXG

    def one_beam(carry, beam):
        tilt_x = tilts[beam, 0]
        tilt_y = tilts[beam, 1]
        phase_x = (tilt_x * cols_all % NXG).astype(jnp.float32) / NXG
        phase_y = (tilt_y * rows_all % NY).astype(jnp.float32) / NY
        plane_angle = 2.0 * math.pi * (phase_y[:, None] + phase_x[None, :])
        plane_re = jnp.cos(plane_angle)
        plane_im = jnp.sin(plane_angle)
        wave_re = (plane_re * trans_real[0] - plane_im * trans_imag[0]).astype(jnp.bfloat16)
        wave_im = (plane_re * trans_imag[0] + plane_im * trans_real[0]).astype(jnp.bfloat16)
        for layer in range(SLICES):
            cross_re, cross_im = convolve(wave_re, wave_im, ft_cols, 1)
            cross_re = cross_re.astype(jnp.bfloat16)
            cross_im = cross_im.astype(jnp.bfloat16)
            down_re, down_im = convolve(cross_re, cross_im, ft_rows, 0)
            if layer + 1 < SLICES:
                wave_re = (down_re * trans_real[layer + 1] - down_im * trans_imag[layer + 1]).astype(jnp.bfloat16)
                wave_im = (down_re * trans_imag[layer + 1] + down_im * trans_real[layer + 1]).astype(jnp.bfloat16)
            else:
                wave_re = down_re.astype(jnp.bfloat16)
                wave_im = down_im.astype(jnp.bfloat16)
        crop_re = wave_re[win_rows[:, :, None], win_cols[:, None, :]].astype(jnp.float32)
        crop_im = wave_im[win_rows[:, :, None], win_cols[:, None, :]].astype(jnp.float32)
        probe_x = (tilt_x * positions[:, 1] % NXG).astype(jnp.float32) / NXG
        probe_y = (tilt_y * positions[:, 0] % NY).astype(jnp.float32) / NY
        probe_angle = -2.0 * math.pi * (probe_y + probe_x)
        coef_re = (aperture[beam] * jnp.cos(probe_angle))[:, None, None]
        coef_im = (aperture[beam] * jnp.sin(probe_angle))[:, None, None]
        psi_re, psi_im = carry
        psi_re = psi_re + coef_re * crop_re - coef_im * crop_im
        psi_im = psi_im + coef_re * crop_im + coef_im * crop_re
        return ((psi_re, psi_im), None)
    zeros_win = jnp.zeros((PROBES, WIN, WIN), jnp.float32)
    (psi_re, psi_im), ignored = lax.scan(one_beam, (zeros_win, zeros_win), jnp.arange(BEAMS, dtype=jnp.int32))
    return ((psi_re * psi_re + psi_im * psi_im) / BEAMS).reshape(PROBES, WIN * WIN)
```

```python
import math

import jax
import jax.numpy as jnp
import ml_dtypes
import numpy as np
from jax import lax
from jax.experimental import pallas as pl
from jax.experimental.pallas import tpu as pltpu
from jax.sharding import PartitionSpec as P

HALFW = 32
TYPES = 4
WIN = 128
LANES = 128
GROUP = 64
HALO0 = 64
HALO1 = 32
TABLE = 384
MIB = 1024 * 1024


def taps(offset):
    steps = np.arange(-HALFW, HALFW + 1, dtype=np.float32)
    weights = 1.0 - 0.5 * (steps / (HALFW + 1.0)) ** 2
    scale = np.sqrt(np.sum(weights * weights))
    offset = offset.astype(np.float32)
    weight = (1.0 - 0.5 * (offset / (HALFW + 1.0)) ** 2) / scale
    chirp = np.float32(math.pi) * offset * offset / np.float32(2.0 * HALFW + 1.0)
    inside = np.abs(offset) <= HALFW
    real = np.where(inside, np.cos(chirp) * weight, 0.0)
    imag = np.where(inside, np.sin(chirp) * weight, 0.0)
    return real.astype(np.float32), imag.astype(np.float32)


def x_matrix(sources, targets):
    rows = []
    for start in range(0, len(sources), LANES):
        src = sources[start : start + LANES]
        real, imag = taps(targets[None, :] - src[:, None] + HALFW)
        rows.append(np.concatenate([real, imag], axis=1))
        rows.append(np.concatenate([-imag, real], axis=1))
    return np.concatenate(rows, axis=0).astype(ml_dtypes.bfloat16)


def y_matrix():
    out = np.arange(GROUP)[:, None]
    src = np.arange(2 * GROUP)[None, :]
    real, imag = taps(out - src + HALFW)
    upper = np.concatenate([real, -imag], axis=1)
    lower = np.concatenate([imag, real], axis=1)
    return np.concatenate([upper, lower], axis=0).astype(ml_dtypes.bfloat16)


def matrices():
    first = x_matrix(np.arange(2 * LANES), np.arange(LANES))
    second = x_matrix(np.arange(LANES, 2 * LANES), np.arange(LANES, 2 * LANES))
    second = second.reshape(2 * LANES, 2, LANES)
    second[:, :, LANES // 2 :] = 0
    return first, second.reshape(2 * LANES, 2 * LANES), y_matrix()


def pack_kernel(place_ref, pos_ref, first_ref, second_ref, out_ref):
    lane = lax.broadcasted_iota(jnp.int32, (16, LANES), 1)
    out_ref[0:HALO0, :] = first_ref[0].astype(jnp.int16)
    out_ref[HALO0 : HALO0 + HALO1, :] = second_ref[0].astype(jnp.int16)
    tail = jnp.zeros((16, LANES), jnp.int32)
    count = pos_ref.shape[0]
    for probe in range(count):
        tail = jnp.where(lane == probe, pos_ref[probe, 0], tail)
        tail = jnp.where(lane == count + probe, pos_ref[probe, 1], tail)
    tail = tail.astype(jnp.int16)
    for start in range(0, out_ref.shape[1], LANES):
        out_ref[HALO0 + HALO1 :, start : start + LANES] = tail


def pack_rows(place, positions, atoms):
    rows, width = atoms.shape[1], atoms.shape[2]
    half = width // 2
    step = 512
    steps = half // step
    last0, last1 = rows // HALO0 - 1, rows // HALO1 - 1
    return pl.pallas_call(
        pack_kernel,
        out_shape=jax.ShapeDtypeStruct((HALO0 + HALO1 + 16, half), jnp.int16),
        grid_spec=pltpu.PrefetchScalarGridSpec(
            num_scalar_prefetch=1,
            grid=(steps,),
            in_specs=[
                pl.BlockSpec(memory_space=pltpu.SMEM),
                pl.BlockSpec((1, HALO0, step), lambda i, at: (0, (1 - at[0]) * last0, at[1] * steps + i)),
                pl.BlockSpec((1, HALO1, step), lambda i, at: (1, (1 - at[0]) * last1, at[1] * steps + i)),
            ],
            out_specs=pl.BlockSpec((HALO0 + HALO1 + 16, step), lambda i, at: (0, i)),
        ),
    )(place, positions, atoms, atoms)


def words_kernel(place_ref, atoms_ref, out_ref):
    upper = place_ref[0] == 1
    for tile in range(out_ref.shape[0]):
        at = slice(tile * LANES, (tile + 1) * LANES)
        codes = [
            atoms_ref[0, g * GROUP : (g + 1) * GROUP, at]
            + TYPES * atoms_ref[1, g * GROUP : (g + 1) * GROUP, at]
            for g in range(3)
        ]
        own = codes[0] | (codes[1] << 8) | (codes[2] << 16)
        low = (codes[0] << 8) | (codes[1] << 16)
        high = codes[1] | (codes[2] << 8)
        out_ref[tile, 0:GROUP, :] = jnp.where(upper, own, low)
        out_ref[tile, GROUP:, :] = jnp.where(upper, high, own)


def own_words(place, atoms):
    rows, width = atoms.shape[1], atoms.shape[2]
    tiles = 4
    return pl.pallas_call(
        words_kernel,
        out_shape=jax.ShapeDtypeStruct((width // LANES, 2 * GROUP, LANES), jnp.int32),
        grid_spec=pltpu.PrefetchScalarGridSpec(
            num_scalar_prefetch=1,
            grid=(width // (tiles * LANES),),
            in_specs=[pl.BlockSpec((2, rows, tiles * LANES), lambda i, at: (0, 0, i))],
            out_specs=pl.BlockSpec((tiles, 2 * GROUP, LANES), lambda i, at: (i, 0, 0)),
        ),
    )(place, atoms)


def probe_kernel(rows_total, width, beam_ref, out_ref):
    beams = beam_ref.shape[0]
    precise = lax.Precision.HIGHEST

    def cos_turns(turns):
        return jnp.cos((2.0 * math.pi) * (turns - jnp.round(turns)))

    lane = lax.broadcasted_iota(jnp.int32, (1, LANES), 1)
    tilt_y = jnp.zeros((1, LANES), jnp.float32)
    for beam in range(beams):
        tilt_y = jnp.where(lane % beams == beam, beam_ref[beam, 1], tilt_y)
    quarter = jnp.where(lane < beams, 0.0, 0.25)
    row = lax.broadcasted_iota(jnp.int32, (TABLE, LANES), 0) - TABLE // 2
    along_y = cos_turns(row.astype(jnp.float32) * tilt_y / rows_total - quarter)
    along_y = jnp.where(lane < 2 * beams, along_y, 0.0)

    sub = lax.broadcasted_iota(jnp.int32, (LANES, 1), 0)
    tilt_x = jnp.zeros((LANES, 1), jnp.float32)
    weight = jnp.zeros((LANES, 1), jnp.float32)
    for beam in range(beams):
        mine = (sub % beams == beam) & (sub < 2 * beams)
        tilt_x = jnp.where(mine, beam_ref[beam, 0], tilt_x)
        weight = jnp.where(mine, beam_ref[beam, 2], weight)
    col = lax.broadcasted_iota(jnp.int32, (LANES, 2 * LANES), 1) - LANES
    turns = col.astype(jnp.float32) * tilt_x / width
    shift = jnp.where(sub < beams, 0.0, 0.25)
    right_re = weight * cos_turns(turns + shift)
    right_im = weight * cos_turns(turns + shift - 0.25)
    for part, right in ((0, right_re), (1, right_im)):
        table = jnp.dot(along_y, right, precision=precise, preferred_element_type=jnp.float32)
        for tile in range(2):
            out_ref[part, tile] = table[:, tile * LANES : (tile + 1) * LANES]


def probe_table(beam_rows, rows_total, width):
    def kernel(beam_ref, out_ref):
        probe_kernel(rows_total, width, beam_ref, out_ref)

    return pl.pallas_call(
        kernel,
        out_shape=jax.ShapeDtypeStruct((2, 2, TABLE, LANES), jnp.float32),
        in_specs=[pl.BlockSpec(memory_space=pltpu.SMEM)],
        out_specs=pl.BlockSpec(memory_space=pltpu.VMEM),
    )(beam_rows)


def main_kernel(
    beams,
    place_ref,
    pos_ref,
    near_ref,
    phase_ref,
    words_in,
    mine_ref,
    other_ref,
    table_ref,
    first_ref,
    second_ref,
    ymat_ref,
    own_ref,
    ext_ref,
    words,
    list_ref,
):
    side, core, row_base, near_base = place_ref[0], place_ref[1], place_ref[2], place_ref[3]
    tiles = words.shape[0]
    half_tiles = tiles // 2
    f32, bf16 = jnp.float32, jnp.bfloat16

    def merge(upper):
        base = GROUP if upper else 0
        sft = 16 if upper else 0
        lo = 0 if upper else GROUP - HALO1
        for source, at in ((mine_ref, core), (other_ref, 1 - core)):
            for tile in range(half_tiles):
                cols = slice(tile * LANES, (tile + 1) * LANES)
                zero = source[0:HALO0, cols].astype(jnp.int32)
                one = source[HALO0 : HALO0 + HALO1, cols].astype(jnp.int32) * TYPES
                pieces = []
                if lo:
                    pieces.append(zero[0:lo])
                pieces.append(zero[lo : lo + HALO1] + one)
                if lo + HALO1 < GROUP:
                    pieces.append(zero[lo + HALO1 :])
                code = jnp.concatenate(pieces, axis=0) << sft
                index = at * half_tiles + tile
                words[index, base : base + GROUP, :] = words_in[index, base : base + GROUP, :] | code
                rest = GROUP - base
                words[index, rest : rest + GROUP, :] = words_in[index, rest : rest + GROUP, :]

    @pl.when(side == 0)
    def _():
        merge(False)

    @pl.when(side == 1)
    def _():
        merge(True)

    def values(layer):
        angle = [jnp.full((8, LANES), phase_ref[layer, t], f32) for t in range(TYPES)]
        return [jnp.cos(a)[0:1] for a in angle], [jnp.sin(a)[0:1] for a in angle]

    cos0, sin0 = values(0)
    cos1, sin1 = values(1)
    lane = lax.broadcasted_iota(jnp.int32, (1, LANES), 1)
    rows64 = (GROUP, LANES)

    def transmission(word, bit, cos_v, sin_v):
        b0 = (word & (1 << bit)) != 0
        b1 = (word & (2 << bit)) != 0
        out = []
        for v in (cos_v, sin_v):
            low = jnp.where(b0, jnp.broadcast_to(v[1], rows64), jnp.broadcast_to(v[0], rows64))
            high = jnp.where(b0, jnp.broadcast_to(v[3], rows64), jnp.broadcast_to(v[2], rows64))
            out.append(jnp.where(b1, high, low))
        return out

    def task(row, col):
        start = jnp.clip(row - GROUP, 0, GROUP)
        delta = start - GROUP * (1 - side) - row + TABLE // 2
        tile0 = col // LANES + tiles - 1
        shift = lax.rem(col, LANES)
        back = lax.rem(LANES - shift, LANES)
        rolled = []
        for j in range(3):
            word = words[lax.rem(tile0 + j, tiles), pl.ds(start, GROUP), :]
            rolled.append(pltpu.roll(word, back, 1))
        keep = lane < LANES - shift
        window = [jnp.where(keep, rolled[j], rolled[j + 1]) for j in range(2)]

        blocks = []
        for g in range(3):
            parts = []
            for j in range(2):
                t_re, t_im = transmission(window[j], 8 * g, cos0, sin0)
                p_re = table_ref[0, j, pl.ds(delta + g * GROUP, GROUP), :]
                p_im = table_ref[1, j, pl.ds(delta + g * GROUP, GROUP), :]
                parts.append((p_re * t_re - p_im * t_im).astype(bf16))
                parts.append((p_re * t_im + p_im * t_re).astype(bf16))
            blocks.append(jnp.concatenate(parts, axis=1))
        wave = jnp.concatenate(blocks, axis=0)
        one = jnp.dot(wave, first_ref[...], preferred_element_type=f32).astype(bf16)
        two = jnp.dot(wave[:, 2 * LANES :], second_ref[...], preferred_element_type=f32).astype(bf16)
        real = jnp.concatenate([one[:, :LANES], two[:, :LANES]], axis=1)
        imag = jnp.concatenate([one[:, LANES:], two[:, LANES:]], axis=1)

        turned = [pltpu.roll(w, LANES - HALFW, 1) for w in window]
        mid = [jnp.where(lane < LANES - HALFW, turned[0], turned[1]), turned[1]]
        blocks = []
        for b in range(2):
            rows = slice(b * GROUP, b * GROUP + 2 * GROUP)
            stacked = jnp.concatenate([real[rows], imag[rows]], axis=0)
            down = jnp.dot(ymat_ref[...], stacked, preferred_element_type=f32)
            parts = []
            for j in range(2):
                cols = slice(j * LANES, (j + 1) * LANES)
                d_re, d_im = down[:GROUP, cols], down[GROUP:, cols]
                word = jnp.concatenate(
                    [mid[j][HALO1:] >> (8 * b), mid[j][:HALO1] >> (8 * b + 8)], axis=0
                )
                t_re, t_im = transmission(word, 2, cos1, sin1)
                parts.append((d_re * t_re - d_im * t_im).astype(bf16))
                parts.append((d_re * t_im + d_im * t_re).astype(bf16))
            blocks.append(jnp.concatenate(parts, axis=1))
        wave = jnp.concatenate(blocks, axis=0)
        one = jnp.dot(wave, first_ref[...], preferred_element_type=f32).astype(bf16)
        stacked = jnp.concatenate([one[:, :LANES], one[:, LANES:]], axis=0)
        exit_wave = jnp.dot(ymat_ref[...], stacked, preferred_element_type=f32)
        exit_wave = exit_wave.astype(bf16).astype(f32)
        re, im = exit_wave[:GROUP], exit_wave[GROUP:]
        return ((re * re + im * im) * (1.0 / beams)).astype(bf16)

    count = own_ref.shape[0]

    def own_step(i, carry):
        for k in (2 * i, 2 * i + 1):
            probe = 2 * k + core
            own_ref[k] = task(pos_ref[probe, 0] - row_base, pos_ref[probe, 1])
        return carry

    lax.fori_loop(0, count // 2, own_step, 0)

    def find(k, found):
        row = near_ref[2 * k + core] - near_base
        reaches = jnp.where(side == 0, row > -GROUP, row < 4 * GROUP)
        list_ref[found] = k
        return found + reaches.astype(jnp.int32)

    found = lax.fori_loop(0, count, find, 0)

    def ext_step(i, carry):
        for k in (2 * i, jnp.minimum(2 * i + 1, found - 1)):
            slot = list_ref[k]
            probe = 2 * slot + core
            ext_ref[slot] = task(near_ref[probe] - near_base, near_ref[2 * count + probe])
        return carry

    lax.fori_loop(0, (found + 1) // 2, ext_step, 0)


def propagate(beams, place, positions, near, phases, words, mine, other, table):
    count = positions.shape[0] // 2
    first, second, ymat = matrices()
    smem = pl.BlockSpec(memory_space=pltpu.SMEM)
    vmem = pl.BlockSpec(memory_space=pltpu.VMEM)

    def kernel(*refs):
        main_kernel(beams, *refs)

    shape = jax.ShapeDtypeStruct((count, GROUP, WIN), jnp.bfloat16)
    return pl.pallas_call(
        kernel,
        out_shape=[shape, shape],
        in_specs=[smem] * 4 + [vmem] * 7,
        out_specs=[vmem, vmem],
        scratch_shapes=[pltpu.VMEM(words.shape, jnp.int32), pltpu.SMEM((count + 1,), jnp.int32)],
        compiler_params=pltpu.CompilerParams(vmem_limit_bytes=40 * MIB),
    )(place, positions, near, phases, words, mine, other, table, first, second, ymat)


def gather_kernel(place_ref, pos_ref, *refs):
    out_ref, column, window = refs[8], refs[9], refs[10]
    side, core, row_base = place_ref[0], place_ref[1], place_ref[2]
    group = pl.program_id(0)
    f32 = jnp.float32
    for par in range(2):
        parity = core if par == 0 else 1 - core
        own, across, below_or_above, far = refs[4 * par : 4 * par + 4]
        for i in range(4):
            at = 8 * group + 2 * i + parity
            row = pos_ref[at, 0] - row_base
            start = jnp.where(row < GROUP, row, jnp.where(row > 2 * GROUP, row - GROUP, GROUP))
            column[pl.ds(pl.multiple_of(GROUP + GROUP * side, GROUP), GROUP), :] = own[i].astype(f32)
            column[pl.ds(pl.multiple_of(2 * GROUP - GROUP * side, GROUP), GROUP), :] = across[i].astype(f32)
            column[pl.ds(pl.multiple_of(3 * GROUP * (1 - side), GROUP), GROUP), :] = below_or_above[i].astype(f32)
            column[pl.ds(pl.multiple_of(3 * GROUP * side, GROUP), GROUP), :] = far[i].astype(f32)
            slot = pl.multiple_of((2 * i + parity) * WIN, WIN)
            window[pl.ds(slot, WIN), :] = column[pl.ds(start, WIN), :]
    for u in range(WIN):
        out_ref[:, u * WIN : (u + 1) * WIN] = window[pl.ds(u, 8, stride=WIN), :]


def put_together(place, positions, pieces):
    probes = positions.shape[0]
    piece = pl.BlockSpec((4, GROUP, WIN), lambda i, *_: (i, 0, 0))
    return pl.pallas_call(
        gather_kernel,
        out_shape=jax.ShapeDtypeStruct((probes, WIN * WIN), jnp.float32),
        grid_spec=pltpu.PrefetchScalarGridSpec(
            num_scalar_prefetch=2,
            grid=(probes // 8,),
            in_specs=[piece] * 8,
            out_specs=pl.BlockSpec((8, WIN * WIN), lambda i, *_: (i, 0)),
            scratch_shapes=[
                pltpu.VMEM((4 * GROUP, LANES), jnp.float32),
                pltpu.VMEM((8 * WIN, LANES), jnp.float32),
            ],
        ),
    )(place, positions, *pieces)


def local(atoms, phases, aperture, tilts, positions):
    rows_here, width = atoms.shape[1], atoms.shape[2]
    probes = positions.shape[0]
    strip, beam = lax.axis_index("strip"), lax.axis_index("beam")
    strips, ways = lax.axis_size("strip"), lax.axis_size("beam")
    rows_total = rows_here * strips
    beams = tilts.shape[0] * ways
    cores = 2
    side, core = beam // cores, beam % cores
    near_strip = jnp.where(side == 0, strip - 1 + strips, strip + 1) % strips
    near_base = near_strip * rows_here + jnp.where(side == 0, rows_here, -rows_here)
    place = jnp.stack([side, core, strip * rows_here, near_base]).astype(jnp.int32)

    def across(array, dest):
        pairs = []
        for s in range(strips):
            for b in range(ways):
                to_s, to_b = dest(s, b // cores, b % cores)
                pairs.append((b * strips + s, (to_b[0] * cores + to_b[1]) * strips + to_s % strips))
        return lax.ppermute(array, ("beam", "strip"), pairs)

    def swap_cores(array):
        return across(array, lambda s, y, c: (s, (y, 1 - c)))

    payload = pack_rows(place, positions, atoms)
    mine = across(payload, lambda s, y, c: (s + 1 - 2 * y, (y, c)))
    beam_rows = jnp.concatenate([tilts.astype(jnp.float32), aperture[:, None]], axis=1)
    beam_rows = lax.all_gather(beam_rows, "beam", axis=0, tiled=True)
    words = own_words(place, atoms)
    table = probe_table(beam_rows, rows_total, width)
    other = swap_cores(mine)
    near = mine[HALO0 + HALO1, : 2 * probes].astype(jnp.int32)
    own, ext = propagate(beams, place, positions, near, phases, words, mine, other, table)
    far = across(ext, lambda s, y, c: (s - 1 + 2 * y, (1 - y, c)))
    same = across(ext, lambda s, y, c: (s - 1 + 2 * y, (y, c)))
    facing = across(own, lambda s, y, c: (s, (1 - y, c)))
    pieces = [own, facing, same, far]
    return put_together(place, positions, pieces + [swap_cores(piece) for piece in pieces])


def solution(mesh):
    in_specs = (P(None, "strip", None), P(), P("beam"), P("beam", None), P("strip", None))
    out_specs = P("strip", None)
    return jax.shard_map(local, mesh=mesh, in_specs=in_specs, out_specs=out_specs, check_vma=False)
```

```python
import math

import jax
import jax.numpy as jnp
import ml_dtypes
import numpy as np
from jax import lax
from jax.experimental import pallas as pl
from jax.experimental.pallas import tpu as pltpu
from jax.sharding import PartitionSpec as P

HALFW = 32
TYPES = 4
WIN = 128
LANES = 128
GROUP = 64
HALO0 = 64
HALO1 = 32
TABLE = 384
MIB = 1024 * 1024


def taps(offset):
    steps = np.arange(-HALFW, HALFW + 1, dtype=np.float32)
    weights = 1.0 - 0.5 * (steps / (HALFW + 1.0)) ** 2
    scale = np.sqrt(np.sum(weights * weights))
    offset = offset.astype(np.float32)
    weight = (1.0 - 0.5 * (offset / (HALFW + 1.0)) ** 2) / scale
    chirp = np.float32(math.pi) * offset * offset / np.float32(2.0 * HALFW + 1.0)
    inside = np.abs(offset) <= HALFW
    real = np.where(inside, np.cos(chirp) * weight, 0.0)
    imag = np.where(inside, np.sin(chirp) * weight, 0.0)
    return real.astype(np.float32), imag.astype(np.float32)


def x_matrix(sources, targets):
    rows = []
    for start in range(0, len(sources), LANES):
        src = sources[start : start + LANES]
        real, imag = taps(targets[None, :] - src[:, None] + HALFW)
        rows.append(np.concatenate([real, imag], axis=1))
        rows.append(np.concatenate([-imag, real], axis=1))
    return np.concatenate(rows, axis=0).astype(ml_dtypes.bfloat16)


def y_matrix():
    out = np.arange(GROUP)[:, None]
    src = np.arange(2 * GROUP)[None, :]
    real, imag = taps(out - src + HALFW)
    upper = np.concatenate([real, -imag], axis=1)
    lower = np.concatenate([imag, real], axis=1)
    return np.concatenate([upper, lower], axis=0).astype(ml_dtypes.bfloat16)


def matrices():
    first = x_matrix(np.arange(2 * LANES), np.arange(LANES))
    second = x_matrix(np.arange(LANES, 2 * LANES), np.arange(LANES, 2 * LANES))
    second = second.reshape(2 * LANES, 2, LANES)
    second[:, :, LANES // 2 :] = 0
    return first, second.reshape(2 * LANES, 2 * LANES), y_matrix()


def pack_kernel(place_ref, atoms_hbm, zero_ref, one_ref, zero_buf, one_buf, sems):
    half = zero_ref.shape[1]
    rows = atoms_hbm.shape[1]
    side, core = place_ref[0], place_ref[1]
    step = half // 2
    copies = []
    for layer, buf in ((0, zero_buf), (1, one_buf)):
        depth = buf.shape[0]
        top = pl.multiple_of((1 - side) * (rows - depth), depth)
        for part in range(2):
            left = pl.multiple_of(core * half + part * step, LANES)
            copies.append(
                pltpu.make_async_copy(
                    atoms_hbm.at[layer, pl.ds(top, depth), pl.ds(left, step)],
                    buf.at[:, pl.ds(part * step, step)],
                    sems.at[2 * layer + part],
                )
            )
    for copy in copies:
        copy.start()
    for layer, (buf, out_ref) in enumerate(((zero_buf, zero_ref), (one_buf, one_ref))):
        for part in range(2):
            copies[2 * layer + part].wait()
            cols = slice(part * step, (part + 1) * step)
            out_ref[:, cols] = buf[:, cols].astype(jnp.int16)


def pack_rows(place, atoms):
    half = atoms.shape[2] // 2
    vmem = pl.BlockSpec(memory_space=pltpu.VMEM)
    return pl.pallas_call(
        pack_kernel,
        out_shape=[jax.ShapeDtypeStruct((depth, half), jnp.int16) for depth in (HALO0, HALO1)],
        in_specs=[pl.BlockSpec(memory_space=pltpu.SMEM), pl.BlockSpec(memory_space=pltpu.HBM)],
        out_specs=[vmem, vmem],
        scratch_shapes=[
            pltpu.VMEM((HALO0, half), jnp.int32),
            pltpu.VMEM((HALO1, half), jnp.int32),
            pltpu.SemaphoreType.DMA((4,)),
        ],
        compiler_params=pltpu.CompilerParams(vmem_limit_bytes=60 * MIB),
    )(place, atoms)


def words_kernel(place_ref, atoms_hbm, out_ref, buf, sems):
    upper = place_ref[0] == 1
    parts = sems.shape[0]
    step = buf.shape[2] // parts
    copies = [
        pltpu.make_async_copy(
            atoms_hbm.at[:, :, pl.ds(k * step, step)], buf.at[:, :, pl.ds(k * step, step)], sems.at[k]
        )
        for k in range(parts)
    ]
    for copy in copies:
        copy.start()
    for k in range(parts):
        copies[k].wait()
        for tile in range(k * step // LANES, (k + 1) * step // LANES):
            at = slice(tile * LANES, (tile + 1) * LANES)
            codes = []
            for g in range(3):
                rows = slice(g * GROUP, (g + 1) * GROUP)
                codes.append(buf[0, rows, at] + TYPES * buf[1, rows, at])
            own = codes[0] | (codes[1] << 8) | (codes[2] << 16)
            low = (codes[0] << 8) | (codes[1] << 16)
            high = codes[1] | (codes[2] << 8)
            out_ref[tile, 0:GROUP, :] = jnp.where(upper, own, low)
            out_ref[tile, GROUP:, :] = jnp.where(upper, high, own)


def own_words(place, atoms):
    width = atoms.shape[2]
    return pl.pallas_call(
        words_kernel,
        out_shape=pltpu.VMEM((width // LANES, 2 * GROUP, LANES), jnp.int32),
        in_specs=[pl.BlockSpec(memory_space=pltpu.SMEM), pl.BlockSpec(memory_space=pltpu.HBM)],
        out_specs=pl.BlockSpec(memory_space=pltpu.VMEM),
        scratch_shapes=[pltpu.VMEM(atoms.shape, jnp.int32), pltpu.SemaphoreType.DMA((8,))],
        compiler_params=pltpu.CompilerParams(vmem_limit_bytes=60 * MIB),
        cost_estimate=pl.CostEstimate(flops=20 * atoms.size, bytes_accessed=6 * atoms.size, transcendentals=0),
    )(place, atoms)


def cos_turns(turns):
    angle = (2.0 * math.pi) * (0.25 - jnp.abs(turns - jnp.round(turns)))
    square = angle * angle
    total = jnp.full_like(square, 1.0)
    for k in (12, 10, 8, 6, 4, 2):
        total = 1.0 - square * total * (1.0 / (k * (k + 1)))
    return angle * total


def probe_kernel(rows_total, width, beam_ref, phase_ref, out_ref, values_ref):
    beams = beam_ref.shape[0]
    precise = lax.Precision.HIGHEST
    lane = lax.broadcasted_iota(jnp.int32, (1, LANES), 1)
    tilt_y = jnp.zeros((1, LANES), jnp.float32)
    for beam in range(beams):
        tilt_y = jnp.where(lane % beams == beam, beam_ref[beam, 1], tilt_y)
    quarter = jnp.where(lane < beams, 0.0, 0.25)
    row = lax.broadcasted_iota(jnp.int32, (TABLE, LANES), 0) - TABLE // 2
    along_y = cos_turns(row.astype(jnp.float32) * tilt_y / rows_total - quarter)
    along_y = jnp.where(lane < 2 * beams, along_y, 0.0)

    sub = lax.broadcasted_iota(jnp.int32, (2 * beams, 1), 0)
    tilt_x = jnp.zeros((2 * beams, 1), jnp.float32)
    weight = jnp.zeros((2 * beams, 1), jnp.float32)
    for beam in range(beams):
        tilt_x = jnp.where(sub % beams == beam, beam_ref[beam, 0], tilt_x)
        weight = jnp.where(sub % beams == beam, beam_ref[beam, 2], weight)
    col = lax.broadcasted_iota(jnp.int32, (2 * beams, 2 * LANES), 1) - LANES
    turns = col.astype(jnp.float32) * tilt_x / width
    shift = jnp.where(sub < beams, 0.0, 0.25)
    right_re = weight * cos_turns(turns + shift)
    right_im = weight * cos_turns(turns + shift - 0.25)
    right = jnp.concatenate([right_re, right_im], axis=1)
    right = jnp.concatenate([right, jnp.zeros((LANES - 2 * beams, 4 * LANES), jnp.float32)], axis=0)
    table = jnp.dot(along_y, right, precision=precise, preferred_element_type=jnp.float32)
    for part in range(2):
        for tile in range(2):
            lo = (2 * part + tile) * LANES
            out_ref[part, tile] = table[:, lo : lo + LANES]

    sub = lax.broadcasted_iota(jnp.int32, (4 * TYPES, LANES), 0)
    angle = jnp.zeros((4 * TYPES, LANES), jnp.float32)
    for layer in range(2):
        for kind in range(TYPES):
            mine = (sub // (2 * TYPES) == layer) & (sub % TYPES == kind)
            angle = jnp.where(mine, phase_ref[layer, kind], angle)
    quarter = jnp.where((sub // TYPES) % 2 == 0, 0.0, 0.25)
    values_ref[...] = cos_turns(angle * (0.5 / math.pi) - quarter)


def probe_table(beam_rows, phases, rows_total, width):
    def kernel(*refs):
        probe_kernel(rows_total, width, *refs)

    smem = pl.BlockSpec(memory_space=pltpu.SMEM)
    vmem = pl.BlockSpec(memory_space=pltpu.VMEM)
    return pl.pallas_call(
        kernel,
        out_shape=[pltpu.VMEM((2, 2, TABLE, LANES), jnp.float32), pltpu.VMEM((4 * TYPES, LANES), jnp.float32)],
        in_specs=[smem, smem],
        out_specs=[vmem, vmem],
        cost_estimate=pl.CostEstimate(flops=10**8, bytes_accessed=10**6, transcendentals=10**5),
    )(beam_rows, phases)


def main_kernel(
    beams,
    place_ref,
    pos_ref,
    near_ref,
    words_in,
    mine0_ref,
    mine1_ref,
    other0_ref,
    other1_ref,
    table_ref,
    values_ref,
    first_ref,
    second_ref,
    ymat_ref,
    own_hbm,
    ext_hbm,
    words,
    left,
    right,
    middle,
    result,
    row_list,
    col_list,
    slot_list,
    sems,
):
    side, core, row_base, near_base = place_ref[0], place_ref[1], place_ref[2], place_ref[3]
    tiles = words.shape[0]
    half_tiles = tiles // 2
    f32, bf16 = jnp.float32, jnp.bfloat16

    def merge(upper):
        base = GROUP if upper else 0
        sft = 16 if upper else 0
        lo = 0 if upper else GROUP - HALO1
        for zeros, ones, at in ((mine0_ref, mine1_ref, core), (other0_ref, other1_ref, 1 - core)):
            for tile in range(half_tiles):
                cols = slice(tile * LANES, (tile + 1) * LANES)
                zero = zeros[:, cols].astype(jnp.int32)
                one = ones[:, cols].astype(jnp.int32) * TYPES
                pieces = []
                if lo:
                    pieces.append(zero[0:lo])
                pieces.append(zero[lo : lo + HALO1] + one)
                if lo + HALO1 < GROUP:
                    pieces.append(zero[lo + HALO1 :])
                code = jnp.concatenate(pieces, axis=0) << sft
                index = at * half_tiles + tile
                words[index, base : base + GROUP, :] = words_in[index, base : base + GROUP, :] | code

    @pl.when(side == 0)
    def _():
        merge(False)

    @pl.when(side == 1)
    def _():
        merge(True)

    def values(layer):
        rows = [values_ref[2 * TYPES * layer + k : 2 * TYPES * layer + k + 1, :].astype(bf16) for k in range(2 * TYPES)]
        return rows[:TYPES], rows[TYPES:]

    cos0, sin0 = values(0)
    cos1, sin1 = values(1)
    lane = lax.broadcasted_iota(jnp.int32, (1, LANES), 1)

    def transmission(code, bit, cos_v, sin_v):
        b0 = (code & jnp.int16(1 << bit)) != 0
        b1 = (code & jnp.int16(2 << bit)) != 0
        out = []
        for v in (cos_v, sin_v):
            spread = [jnp.broadcast_to(value, code.shape) for value in v]
            out.append(jnp.where(b1, jnp.where(b0, spread[3], spread[2]), jnp.where(b0, spread[1], spread[0])))
        return out

    def probe_window(t, buf, mid_buf):
        row, col = row_list[t], col_list[t]
        start = jnp.clip(row - GROUP, 0, GROUP)
        delta = start - GROUP * (1 - side) - row + TABLE // 2
        tile0 = col // LANES + tiles - 1
        shift = lax.rem(col, LANES)
        back = lax.rem(LANES - shift, LANES)
        rolled = []
        for j in range(3):
            word = words[lax.rem(tile0 + j, tiles), pl.ds(start, GROUP), :]
            rolled.append(pltpu.roll(word, back, 1))
        keep = lane < LANES - shift
        window = [jnp.where(keep, rolled[j], rolled[j + 1]) for j in range(2)]
        turned = [pltpu.roll(w, LANES - HALFW, 1) for w in window]
        inner = [jnp.where(lane < LANES - HALFW, turned[0], turned[1]), turned[1]]
        for j in range(2):
            mid_buf[j, 0] = inner[j].astype(jnp.int16)
            mid_buf[j, 1] = (inner[j] >> 16).astype(jnp.int16)
            codes = (window[j].astype(jnp.int16), (window[j] >> 16).astype(jnp.int16))
            for g in range(3):
                t_re, t_im = transmission(codes[g // 2], 8 * (g % 2), cos0, sin0)
                p_re = table_ref[0, j, pl.ds(delta + g * GROUP, GROUP), :].astype(bf16)
                p_im = table_ref[1, j, pl.ds(delta + g * GROUP, GROUP), :].astype(bf16)
                at = slice(g * GROUP, (g + 1) * GROUP)
                lo = 2 * j * LANES
                buf[at, lo : lo + LANES] = p_re * t_re - p_im * t_im
                buf[at, lo + LANES : lo + 2 * LANES] = p_re * t_im + p_im * t_re

    count = own_hbm.shape[0]

    def own_task(k, carry):
        probe = 2 * k + core
        row_list[k] = pos_ref[probe, 0] - row_base
        col_list[k] = pos_ref[probe, 1]
        slot_list[k] = k
        return carry

    def ext_task(k, found):
        probe = 2 * k + core
        row = near_ref[probe, 0] - near_base
        reaches = jnp.where(side == 0, row > -GROUP, row < 4 * GROUP)
        row_list[found] = row
        col_list[found] = near_ref[probe, 1]
        slot_list[found] = count + k
        return found + reaches.astype(jnp.int32)

    lax.fori_loop(0, count, own_task, 0)
    total = lax.fori_loop(0, count, ext_task, count)

    def step(t, p):
        q = 1 - p
        one = jnp.dot(left[q], first_ref[...], preferred_element_type=f32).astype(bf16)
        two = jnp.dot(left[q, : 3 * GROUP, 2 * LANES :], second_ref[...], preferred_element_type=f32)
        two = two.astype(bf16)
        down = jnp.dot(ymat_ref[...], right[p], preferred_element_type=f32)
        for part in range(2):
            to = slice(2 * GROUP * part, 2 * GROUP * (part + 1))
            cols = slice(part * LANES, (part + 1) * LANES)
            for b in range(2):
                rows = slice(b * GROUP, b * GROUP + 2 * GROUP)
                right[q, to, 2 * b * LANES : (2 * b + 1) * LANES] = one[rows, cols]
                right[q, to, (2 * b + 1) * LANES : (2 * b + 2) * LANES] = two[rows, cols]
            right[q, to, 4 * LANES :] = one[3 * GROUP :, cols]
        for b in range(2):
            for j in range(2):
                lo = (2 * b + j) * LANES
                cols = slice(2 * j * LANES, (2 * j + 1) * LANES)
                imag_cols = slice((2 * j + 1) * LANES, (2 * j + 2) * LANES)
                for part in range(2):
                    group = b + part
                    code = middle[p, j, group // 2, (1 - part) * HALO1 : (2 - part) * HALO1]
                    t_re, t_im = transmission(code, 8 * (group % 2) + 2, cos1, sin1)
                    d_re = down[part * HALO1 : (part + 1) * HALO1, lo : lo + LANES].astype(bf16)
                    d_im = down[GROUP + part * HALO1 : GROUP + (part + 1) * HALO1, lo : lo + LANES].astype(bf16)
                    first_row = (3 + b) * GROUP + part * HALO1
                    rows = slice(first_row, first_row + HALO1)
                    left[p, rows, cols] = d_re * t_re - d_im * t_im
                    left[p, rows, imag_cols] = d_re * t_im + d_im * t_re
        exit_wave = down[:, 4 * LANES :].astype(bf16).astype(f32)
        re, im = exit_wave[:GROUP], exit_wave[GROUP:]
        slot = slot_list[jnp.clip(t - 4, 0, total - 1)]
        result[slot] = ((re * re + im * im) * (1.0 / beams)).astype(bf16)
        probe_window(jnp.minimum(t, total - 1), left.at[p], middle.at[p])

    def steps(i, carry):
        step(2 * i, 0)
        step(2 * i + 1, 1)
        return carry

    lax.fori_loop(0, (total + 5) // 2, steps, 0)
    copies = [
        pltpu.make_async_copy(result.at[pl.ds(0, count)], own_hbm, sems.at[0]),
        pltpu.make_async_copy(result.at[pl.ds(count, count)], ext_hbm, sems.at[1]),
    ]
    for copy in copies:
        copy.start()
    for copy in copies:
        copy.wait()


def propagate(beams, place, positions, near, words, halo, table):
    count = positions.shape[0] // 2
    first, second, ymat = matrices()
    smem = pl.BlockSpec(memory_space=pltpu.SMEM)
    vmem = pl.BlockSpec(memory_space=pltpu.VMEM)
    hbm = pl.BlockSpec(memory_space=pltpu.HBM)

    def kernel(*refs):
        main_kernel(beams, *refs)

    shape = jax.ShapeDtypeStruct((count, GROUP, WIN), jnp.bfloat16)
    own, ext, _ = pl.pallas_call(
        kernel,
        out_shape=[shape, shape, pltpu.VMEM(words.shape, jnp.int32)],
        in_specs=[smem] * 3 + [vmem] * 10,
        out_specs=[hbm, hbm, vmem],
        input_output_aliases={3: 2},
        scratch_shapes=[
            pltpu.VMEM((2, 5 * GROUP, 4 * LANES), jnp.bfloat16),
            pltpu.VMEM((2, 4 * GROUP, 5 * LANES), jnp.bfloat16),
            pltpu.VMEM((2, 2, 2, GROUP, LANES), jnp.int16),
            pltpu.VMEM((2 * count, GROUP, WIN), jnp.bfloat16),
            pltpu.SMEM((2 * count + 1,), jnp.int32),
            pltpu.SMEM((2 * count + 1,), jnp.int32),
            pltpu.SMEM((2 * count + 1,), jnp.int32),
            pltpu.SemaphoreType.DMA((2,)),
        ],
        compiler_params=pltpu.CompilerParams(vmem_limit_bytes=40 * MIB),
    )(place, positions, near, words, *halo, *table, first, second, ymat)
    return own, ext


PAD = 3 * WIN


def gather_kernel(place_ref, pos_ref, *refs):
    out_hbm, window, out_buf, sems = refs[8:]
    side, core, row_base = place_ref[0], place_ref[1], place_ref[2]

    def copy(group):
        rows = pl.ds(pl.multiple_of(8 * group, 8), 8)
        return pltpu.make_async_copy(out_buf.at[rows], out_hbm.at[rows], sems.at[group])

    def step(group, carry):
        for par in range(2):
            parity = core if par == 0 else 1 - core
            for i in range(4):
                k = 4 * group + i
                row = pos_ref[2 * k + parity, 0] - row_base
                start = jnp.where(row < GROUP, row, jnp.where(row > 2 * GROUP, row - GROUP, GROUP))
                base = (2 * i + parity) * PAD + WIN - start
                places = (GROUP + GROUP * side, 2 * GROUP - GROUP * side, 3 * GROUP * (1 - side), 3 * GROUP * side)
                for piece, at in zip(refs[4 * par : 4 * par + 4], places):
                    window[pl.ds(base + at, GROUP), :] = piece[k].astype(jnp.float32)
        rows = pl.ds(pl.multiple_of(8 * group, 8), 8)
        for u in range(WIN):
            out_buf[rows, u * WIN : (u + 1) * WIN] = window[pl.ds(WIN + u, 8, stride=PAD), :]
        copy(group).start()
        return carry

    groups = out_buf.shape[0] // 8
    lax.fori_loop(0, groups, step, 0)
    for group in range(groups):
        copy(group).wait()


def put_together(place, positions, pieces):
    probes = positions.shape[0]
    smem = pl.BlockSpec(memory_space=pltpu.SMEM)
    vmem = pl.BlockSpec(memory_space=pltpu.VMEM)
    return pl.pallas_call(
        gather_kernel,
        out_shape=jax.ShapeDtypeStruct((probes, WIN * WIN), jnp.float32),
        in_specs=[smem, smem] + [vmem] * 8,
        out_specs=pl.BlockSpec(memory_space=pltpu.HBM),
        scratch_shapes=[
            pltpu.VMEM((8 * PAD, LANES), jnp.float32),
            pltpu.VMEM((probes, WIN * WIN), jnp.float32),
            pltpu.SemaphoreType.DMA((probes // 8,)),
        ],
        compiler_params=pltpu.CompilerParams(vmem_limit_bytes=16 * MIB),
    )(place, positions, *pieces)


def local(atoms, phases, aperture, tilts, positions):
    rows_here, width = atoms.shape[1], atoms.shape[2]
    probes = positions.shape[0]
    strip, beam = lax.axis_index("strip"), lax.axis_index("beam")
    strips, ways = lax.axis_size("strip"), lax.axis_size("beam")
    rows_total = rows_here * strips
    beams = tilts.shape[0] * ways
    cores = 2
    side, core = beam // cores, beam % cores
    near_strip = jnp.where(side == 0, strip - 1 + strips, strip + 1) % strips
    near_base = near_strip * rows_here + jnp.where(side == 0, rows_here, -rows_here)
    place = jnp.stack([side, core, strip * rows_here, near_base]).astype(jnp.int32)

    def across(array, dest):
        pairs = []
        for s in range(strips):
            for b in range(ways):
                to_s, to_b = dest(s, b // cores, b % cores)
                pairs.append((b * strips + s, (to_b[0] * cores + to_b[1]) * strips + to_s % strips))
        return lax.ppermute(array, ("beam", "strip"), pairs)

    def swap_cores(array):
        return across(array, lambda s, y, c: (s, (y, 1 - c)))

    packed = pack_rows(place, atoms)
    mine = [across(rows, lambda s, y, c: (s + 1 - 2 * y, (y, c))) for rows in packed]
    packed, positions, tilts, aperture = lax.optimization_barrier((packed, positions, tilts, aperture))
    near = across(positions, lambda s, y, c: (s + 1 - 2 * y, (y, c)))
    beam_rows = jnp.concatenate([tilts.astype(jnp.float32), aperture[:, None]], axis=1)
    beam_rows = [
        beam_rows,
        swap_cores(beam_rows),
        across(beam_rows, lambda s, y, c: (s, (1 - y, c))),
        across(beam_rows, lambda s, y, c: (s, (1 - y, 1 - c))),
    ]
    beam_rows = jnp.concatenate(beam_rows, axis=0)
    words = own_words(place, atoms)
    table = probe_table(beam_rows, phases, rows_total, width)
    mine, near, words, table = lax.optimization_barrier((mine, near, words, table))
    other = [swap_cores(rows) for rows in mine]
    halo = mine + other
    own, ext = propagate(beams, place, positions, near, words, halo, table)
    far = across(ext, lambda s, y, c: (s - 1 + 2 * y, (1 - y, c)))
    same = across(ext, lambda s, y, c: (s - 1 + 2 * y, (y, c)))
    facing = across(own, lambda s, y, c: (s, (1 - y, c)))
    pieces = [own, facing, same, far]
    return put_together(place, positions, pieces + [swap_cores(piece) for piece in pieces])


def solution(mesh):
    in_specs = (P(None, "strip", None), P(), P("beam"), P("beam", None), P("strip", None))
    out_specs = P("strip", None)
    return jax.shard_map(local, mesh=mesh, in_specs=in_specs, out_specs=out_specs, check_vma=False)
```

```python
import math

import jax
import jax.numpy as jnp
import ml_dtypes
import numpy as np
from jax import lax
from jax.experimental import pallas as pl
from jax.experimental.pallas import tpu as pltpu
from jax.sharding import PartitionSpec as P

HALFW = 32
TYPES = 4
WIN = 128
LANES = 128
GROUP = 64
PACK = 32
GROUPS = 6
BITS = 4
HALO0 = 64
HALO1 = 32
TABLE = 384
MIB = 1024 * 1024
CORES = 2


def taps(offset):
    steps = np.arange(-HALFW, HALFW + 1, dtype=np.float32)
    weights = 1.0 - 0.5 * (steps / (HALFW + 1.0)) ** 2
    scale = np.sqrt(np.sum(weights * weights))
    offset = offset.astype(np.float32)
    weight = (1.0 - 0.5 * (offset / (HALFW + 1.0)) ** 2) / scale
    chirp = np.float32(math.pi) * offset * offset / np.float32(2.0 * HALFW + 1.0)
    inside = np.abs(offset) <= HALFW
    real = np.where(inside, np.cos(chirp) * weight, 0.0)
    imag = np.where(inside, np.sin(chirp) * weight, 0.0)
    return real.astype(np.float32), imag.astype(np.float32)


def x_matrix(sources, targets):
    rows = []
    for start in range(0, len(sources), LANES):
        src = sources[start : start + LANES]
        real, imag = taps(targets[None, :] - src[:, None] + HALFW)
        rows.append(np.concatenate([real, imag], axis=1))
        rows.append(np.concatenate([-imag, real], axis=1))
    return np.concatenate(rows, axis=0).astype(ml_dtypes.bfloat16)


def y_matrix():
    out = np.arange(GROUP)[:, None]
    src = np.arange(2 * GROUP)[None, :]
    real, imag = taps(out - src + HALFW)
    upper = np.concatenate([real, -imag], axis=1)
    lower = np.concatenate([imag, real], axis=1)
    return np.concatenate([upper, lower], axis=0).astype(ml_dtypes.bfloat16)


def matrices():
    first = x_matrix(np.arange(2 * LANES), np.arange(LANES))
    second = x_matrix(np.arange(LANES, 2 * LANES), np.arange(LANES, 2 * LANES))
    second = second.reshape(2 * LANES, 2, LANES)
    second[:, :, LANES // 2 :] = 0
    return first, second.reshape(2 * LANES, 2 * LANES), y_matrix()


def pack_kernel(atoms_hbm, pos_ref, out_ref, zero_buf, one_buf, pos_buf, sems):
    half = zero_buf.shape[1]
    rows = atoms_hbm.shape[1]
    beam = lax.axis_index("beam")
    side, core = beam // CORES, beam % CORES
    parts = sems.shape[0] // 2
    step = half // parts
    copies = []
    for layer, buf in ((0, zero_buf), (1, one_buf)):
        depth = buf.shape[0]
        top = pl.multiple_of((1 - side) * (rows - depth), depth)
        for part in range(parts):
            left = pl.multiple_of(core * half + part * step, LANES)
            copies.append(
                pltpu.make_async_copy(
                    atoms_hbm.at[layer, pl.ds(top, depth), pl.ds(left, step)],
                    buf.at[:, pl.ds(part * step, step)],
                    sems.at[parts * layer + part],
                )
            )
    for copy in copies:
        copy.start()
    pos_buf[...] = jnp.zeros(pos_buf.shape, jnp.int32)
    pos_buf[:2, : pos_ref.shape[1]] = pos_ref[...]
    out_ref[:16, half:] = pos_buf[...].astype(jnp.int16)
    for layer, (buf, first) in enumerate(((zero_buf, 0), (one_buf, HALO0))):
        for part in range(parts):
            copies[parts * layer + part].wait()
            cols = slice(part * step, (part + 1) * step)
            out_ref[first : first + buf.shape[0], cols] = buf[:, cols].astype(jnp.int16)


def pack_rows(atoms, positions):
    half = atoms.shape[2] // CORES
    vmem = pl.BlockSpec(memory_space=pltpu.VMEM)
    return pl.pallas_call(
        pack_kernel,
        out_shape=pltpu.VMEM((HALO0 + HALO1, half + LANES), jnp.int16),
        in_specs=[pl.BlockSpec(memory_space=pltpu.HBM), vmem],
        out_specs=vmem,
        scratch_shapes=[
            pltpu.VMEM((HALO0, half), jnp.int32),
            pltpu.VMEM((HALO1, half), jnp.int32),
            pltpu.VMEM((16, LANES), jnp.int32),
            pltpu.SemaphoreType.DMA((4,)),
        ],
        compiler_params=pltpu.CompilerParams(vmem_limit_bytes=60 * MIB),
    )(atoms, positions)


def words_kernel(place_ref, atoms_hbm, out_ref, buf, sems):
    upper = place_ref[0] == 1
    parts = sems.shape[0]
    step = buf.shape[2] // parts
    copies = [
        pltpu.make_async_copy(
            atoms_hbm.at[:, :, pl.ds(k * step, step)], buf.at[:, :, pl.ds(k * step, step)], sems.at[k]
        )
        for k in range(parts)
    ]
    for copy in copies:
        copy.start()
    depth = out_ref.shape[1]
    for k in range(parts):
        copies[k].wait()
        for tile in range(k * step // LANES, (k + 1) * step // LANES):
            at = slice(tile * LANES, (tile + 1) * LANES)
            code = buf[0, :, at] + TYPES * buf[1, :, at]
            blocks = [code[n * PACK : (n + 1) * PACK] for n in range(buf.shape[1] // PACK)]
            halo = HALO0 // PACK
            for w in range(depth // PACK):
                words = []
                for first in (halo, 0):
                    word = None
                    for g in range(GROUPS):
                        block = w + g - first
                        if 0 <= block < len(blocks):
                            term = blocks[block] << (BITS * g)
                            word = term if word is None else word | term
                    words.append(word)
                out_ref[tile, w * PACK : (w + 1) * PACK, :] = jnp.where(upper, words[1], words[0])


def own_words(place, atoms):
    width = atoms.shape[2]
    return pl.pallas_call(
        words_kernel,
        out_shape=pltpu.VMEM((width // LANES, GROUP + PACK, LANES), jnp.int32),
        in_specs=[pl.BlockSpec(memory_space=pltpu.SMEM), pl.BlockSpec(memory_space=pltpu.HBM)],
        out_specs=pl.BlockSpec(memory_space=pltpu.VMEM),
        scratch_shapes=[pltpu.VMEM(atoms.shape, jnp.int32), pltpu.SemaphoreType.DMA((8,))],
        compiler_params=pltpu.CompilerParams(vmem_limit_bytes=60 * MIB),
        cost_estimate=pl.CostEstimate(flops=20 * atoms.size, bytes_accessed=6 * atoms.size, transcendentals=0),
    )(place, atoms)


def cos_turns(turns):
    angle = (2.0 * math.pi) * (0.25 - jnp.abs(turns - jnp.round(turns)))
    square = angle * angle
    total = jnp.full_like(square, 1.0)
    for k in (12, 10, 8, 6, 4, 2):
        total = 1.0 - square * total * (1.0 / (k * (k + 1)))
    return angle * total


def probe_kernel(rows_total, width, beam_ref, phase_ref, *refs):
    matrices_hbm, (out_ref, values_ref), matrices_ref, sems = refs[:3], refs[3:5], refs[5:8], refs[8]
    copies = [pltpu.make_async_copy(a, b, sems.at[n]) for n, (a, b) in enumerate(zip(matrices_hbm, matrices_ref))]
    for copy in copies:
        copy.start()
    beams = beam_ref.shape[0]
    precise = lax.Precision.HIGHEST
    lane = lax.broadcasted_iota(jnp.int32, (1, LANES), 1)
    tilt_y = jnp.zeros((1, LANES), jnp.float32)
    for beam in range(beams):
        tilt_y = jnp.where(lane % beams == beam, beam_ref[beam, 1], tilt_y)
    quarter = jnp.where(lane < beams, 0.0, 0.25)
    row = lax.broadcasted_iota(jnp.int32, (TABLE, LANES), 0) - TABLE // 2
    along_y = cos_turns(row.astype(jnp.float32) * tilt_y / rows_total - quarter)
    along_y = jnp.where(lane < 2 * beams, along_y, 0.0)

    sub = lax.broadcasted_iota(jnp.int32, (2 * beams, 1), 0)
    tilt_x = jnp.zeros((2 * beams, 1), jnp.float32)
    weight = jnp.zeros((2 * beams, 1), jnp.float32)
    for beam in range(beams):
        tilt_x = jnp.where(sub % beams == beam, beam_ref[beam, 0], tilt_x)
        weight = jnp.where(sub % beams == beam, beam_ref[beam, 2], weight)
    col = lax.broadcasted_iota(jnp.int32, (2 * beams, 2 * LANES), 1) - LANES
    turns = col.astype(jnp.float32) * tilt_x / width
    shift = jnp.where(sub < beams, 0.0, 0.25)
    right_re = weight * cos_turns(turns + shift)
    right_im = weight * cos_turns(turns + shift - 0.25)
    right = jnp.concatenate([right_re, right_im], axis=1)
    right = jnp.concatenate([right, jnp.zeros((LANES - 2 * beams, 4 * LANES), jnp.float32)], axis=0)
    table = jnp.dot(along_y, right, precision=precise, preferred_element_type=jnp.float32)
    for part in range(2):
        for tile in range(2):
            lo = (2 * part + tile) * LANES
            out_ref[part, tile] = table[:, lo : lo + LANES]

    sub = lax.broadcasted_iota(jnp.int32, (4 * TYPES, LANES), 0)
    angle = jnp.zeros((4 * TYPES, LANES), jnp.float32)
    for layer in range(2):
        for kind in range(TYPES):
            mine = (sub // (2 * TYPES) == layer) & (sub % TYPES == kind)
            angle = jnp.where(mine, phase_ref[layer, kind], angle)
    quarter = jnp.where((sub // TYPES) % 2 == 0, 0.0, 0.25)
    values_ref[...] = cos_turns(angle * (0.5 / math.pi) - quarter)
    for copy in copies:
        copy.wait()


def probe_table(beam_rows, phases, rows_total, width):
    bands = matrices()

    def kernel(*refs):
        probe_kernel(rows_total, width, *refs)

    smem = pl.BlockSpec(memory_space=pltpu.SMEM)
    vmem = pl.BlockSpec(memory_space=pltpu.VMEM)
    return pl.pallas_call(
        kernel,
        out_shape=[pltpu.VMEM((2, 2, TABLE, LANES), jnp.float32), pltpu.VMEM((4 * TYPES, LANES), jnp.float32)]
        + [pltpu.VMEM(matrix.shape, jnp.bfloat16) for matrix in bands],
        in_specs=[smem, smem] + [pl.BlockSpec(memory_space=pltpu.HBM)] * 3,
        out_specs=[vmem] * 5,
        scratch_shapes=[pltpu.SemaphoreType.DMA((3,))],
        compiler_params=pltpu.CompilerParams(vmem_limit_bytes=60 * MIB),
        cost_estimate=pl.CostEstimate(flops=10**8, bytes_accessed=10**6, transcendentals=10**5),
    )(beam_rows, phases, *bands)


def merge_rows(side, core, halo_refs, words_in, words):
    half_tiles = words.shape[0] // CORES

    depth = words.shape[1]

    def merge(upper):
        top = PACK * GROUPS + GROUP - HALO0 if upper else 0
        lo = 0 if upper else HALO0 - HALO1
        for source, at in zip(halo_refs, (core, 1 - core)):
            for tile in range(half_tiles):
                cols = slice(tile * LANES, (tile + 1) * LANES)
                zero = source[:HALO0, cols].astype(jnp.int32)
                one = source[HALO0:, cols].astype(jnp.int32) * TYPES
                blocks = [zero[:PACK], zero[PACK:]]
                blocks[lo // PACK] = blocks[lo // PACK] + one
                index = at * half_tiles + tile
                for w in range(depth // PACK):
                    word = None
                    for g in range(GROUPS):
                        block = w + g - top // PACK
                        if 0 <= block < 2:
                            term = blocks[block] << (BITS * g)
                            word = term if word is None else word | term
                    if word is not None:
                        rows = slice(w * PACK, (w + 1) * PACK)
                        words[index, rows, :] = words_in[index, rows, :] | word

    @pl.when(side == 0)
    def _():
        merge(False)

    @pl.when(side == 1)
    def _():
        merge(True)


def run_tasks(beams, batch_size, side, total, words, table_ref, values_ref, first_ref, second_ref, ymat_ref, result, scratch):
    left, crossed, right, codes_new, codes_old, row_list, col_list, slot_list = scratch
    tiles = words.shape[0]
    f32, bf16, i16 = jnp.float32, jnp.bfloat16, jnp.int16

    def values(layer):
        rows = [values_ref[2 * TYPES * layer + k : 2 * TYPES * layer + k + 1, :].astype(bf16) for k in range(2 * TYPES)]
        return rows[:TYPES], rows[TYPES:]

    cos0, sin0 = values(0)
    cos1, sin1 = values(1)
    lane = lax.broadcasted_iota(jnp.int32, (1, LANES), 1)

    def transmission(code, bit, cos_v, sin_v):
        b0 = (code & i16(1 << bit)) != 0
        b1 = (code & i16(2 << bit if bit < 14 else -(1 << 15))) != 0
        out = []
        for v in (cos_v, sin_v):
            spread = [jnp.broadcast_to(value, code.shape) for value in v]
            out.append(jnp.where(b1, jnp.where(b0, spread[3], spread[2]), jnp.where(b0, spread[1], spread[0])))
        return out

    def split(word):
        return word.astype(i16), (word >> 16).astype(i16)

    def tile_cols(j, part):
        return slice((2 * j + part) * LANES, (2 * j + part + 1) * LANES)

    def waves(batch):
        for k in range(batch_size):
            at = jnp.minimum(batch_size * batch + k, total - 1)
            row, col = row_list[at], col_list[at]
            start = jnp.clip(row - GROUP, 0, GROUP)
            delta = start - GROUP * (1 - side) - row + TABLE // 2
            tile0 = col // LANES + tiles - 1
            shift = lax.rem(col, LANES)
            back = lax.rem(LANES - shift, LANES)
            rolled = []
            for j in range(3):
                word = words[lax.rem(tile0 + j, tiles), pl.ds(start, PACK), :]
                rolled.append(pltpu.roll(word, back, 1))
            keep = lane < LANES - shift
            window = [jnp.where(keep, rolled[j], rolled[j + 1]) for j in range(2)]
            turned = [pltpu.roll(w, LANES - HALFW, 1) for w in window]
            inner = [jnp.where(lane < LANES - HALFW, turned[0], turned[1]), turned[1]]
            for j in range(2):
                codes_new[k, j, 0], codes_new[k, j, 1] = split(inner[j])
                codes = split(window[j])
                for g in range(GROUPS):
                    t_re, t_im = transmission(codes[g // 4], BITS * (g % 4), cos0, sin0)
                    p_re = table_ref[0, j, pl.ds(delta + g * PACK, PACK), :].astype(bf16)
                    p_im = table_ref[1, j, pl.ds(delta + g * PACK, PACK), :].astype(bf16)
                    rows = slice(k * 3 * GROUP + g * PACK, k * 3 * GROUP + (g + 1) * PACK)
                    left[rows, tile_cols(j, 0)] = p_re * t_re - p_im * t_im
                    left[rows, tile_cols(j, 1)] = p_re * t_im + p_im * t_re
        for k in range(batch_size):
            rows = slice(k * 3 * GROUP, (k + 1) * 3 * GROUP)
            one = jnp.dot(left[rows, :], first_ref[...], preferred_element_type=f32).astype(bf16)
            two = jnp.dot(left[rows, 2 * LANES :], second_ref[...], preferred_element_type=f32).astype(bf16)
            for part in range(2):
                cols = slice(part * LANES, (part + 1) * LANES)
                crossed[k, part, :, :LANES] = one[:, cols]
                crossed[k, part, :, LANES:] = two[:, cols]

    def stack(k, b):
        rows = slice(b * GROUP, b * GROUP + 2 * GROUP)
        return jnp.concatenate([crossed[k, part, rows] for part in range(2)], axis=0)

    def rest(batch):
        for k in range(batch_size):
            for b in range(2):
                down = jnp.dot(ymat_ref[...], stack(k, b), preferred_element_type=f32)
                for j in range(2):
                    cols = slice(j * LANES, (j + 1) * LANES)
                    for part in range(2):
                        group = 2 * b + part + 1
                        t_re, t_im = transmission(codes_old[k, j, group // 4], BITS * (group % 4) + 2, cos1, sin1)
                        d_re = down[part * PACK : (part + 1) * PACK, cols].astype(bf16)
                        d_im = down[GROUP + part * PACK : GROUP + (part + 1) * PACK, cols].astype(bf16)
                        top = (2 * k + b) * GROUP + part * PACK
                        right[top : top + PACK, tile_cols(j, 0)] = d_re * t_re - d_im * t_im
                        right[top : top + PACK, tile_cols(j, 1)] = d_re * t_im + d_im * t_re
        one = jnp.dot(right[...], first_ref[...], preferred_element_type=f32).astype(bf16)
        stacks = []
        for k in range(batch_size):
            rows = slice(2 * k * GROUP, (2 * k + 2) * GROUP)
            stacks.append(jnp.concatenate([one[rows, :LANES], one[rows, LANES:]], axis=0))
        exit_waves = jnp.dot(ymat_ref[...], jnp.concatenate(stacks, axis=1), preferred_element_type=f32)
        exit_waves = exit_waves.astype(bf16).astype(f32)
        for k in range(batch_size):
            cols = slice(k * LANES, (k + 1) * LANES)
            re, im = exit_waves[:GROUP, cols], exit_waves[GROUP:, cols]
            slot = slot_list[jnp.minimum(batch_size * batch + k, total - 1)]
            result[slot] = ((re * re + im * im) * (1.0 / beams)).astype(bf16)

    def step(batch, carry):
        rest(batch - 1)
        waves(batch)
        codes_old[...] = codes_new[...]
        return carry

    batches = (total + batch_size - 1) // batch_size
    waves(0)
    codes_old[...] = codes_new[...]
    lax.fori_loop(1, batches, step, 0)
    rest(batches - 1)


def ext_kernel(beams, batch_size, place_ref, near_ref, words_in, mine_ref, other_ref, *refs):
    constants, (out_ref, words), scratch = refs[:5], refs[5:7], refs[7:]
    row_list, col_list, slot_list = scratch[5:]
    side, core, near_base = place_ref[0], place_ref[1], place_ref[3]
    merge_rows(side, core, (mine_ref, other_ref), words_in, words)

    def add(k, found):
        probe = CORES * k + core
        row = near_ref[0, probe] - near_base
        reaches = jnp.where(side == 0, row > -GROUP, row < 4 * GROUP)
        row_list[found] = row
        col_list[found] = near_ref[1, probe]
        slot_list[found] = k
        return found + reaches.astype(jnp.int32)

    total = lax.fori_loop(0, out_ref.shape[0], add, 0)

    @pl.when(total > 0)
    def _():
        run_tasks(beams, batch_size, side, total, words, *constants, out_ref, scratch)


def own_kernel(beams, batch_size, place_ref, pos_ref, words, *refs):
    constants, out_ref, scratch = refs[:5], refs[5], refs[6:]
    row_list, col_list, slot_list = scratch[5:]
    side, core, row_base = place_ref[0], place_ref[1], place_ref[2]
    count = out_ref.shape[0]

    def add(k, carry):
        probe = CORES * k + core
        row_list[k] = pos_ref[0, probe] - row_base
        col_list[k] = pos_ref[1, probe]
        slot_list[k] = k
        return carry

    lax.fori_loop(0, count, add, 0)
    run_tasks(beams, batch_size, side, count, words, *constants, out_ref, scratch)


def propagate(beams, place, probes, words, halo, constants):
    count = probes.shape[1] // CORES
    smem = pl.BlockSpec(memory_space=pltpu.SMEM)
    vmem = pl.BlockSpec(memory_space=pltpu.VMEM)
    ext = bool(halo)
    body = ext_kernel if ext else own_kernel
    batch_size = 4 if ext else count

    def kernel(*refs):
        body(beams, batch_size, *refs)

    shape = jax.ShapeDtypeStruct((count, GROUP, WIN), jnp.bfloat16)
    return pl.pallas_call(
        kernel,
        out_shape=[shape, pltpu.VMEM(words.shape, jnp.int32)] if ext else shape,
        in_specs=[smem] * 2 + [vmem] * (8 if ext else 6),
        out_specs=[vmem, vmem] if ext else vmem,
        input_output_aliases={2: 1} if ext else {},
        scratch_shapes=[
            pltpu.VMEM((batch_size * 3 * GROUP, 4 * LANES), jnp.bfloat16),
            pltpu.VMEM((batch_size, 2, 3 * GROUP, 2 * LANES), jnp.bfloat16),
            pltpu.VMEM((batch_size * 2 * GROUP, 4 * LANES), jnp.bfloat16),
            pltpu.VMEM((batch_size, 2, 2, PACK, LANES), jnp.int16),
            pltpu.VMEM((batch_size, 2, 2, PACK, LANES), jnp.int16),
            pltpu.SMEM((count + 1,), jnp.int32),
            pltpu.SMEM((count + 1,), jnp.int32),
            pltpu.SMEM((count + 1,), jnp.int32),
        ],
        compiler_params=pltpu.CompilerParams(vmem_limit_bytes=40 * MIB),
        cost_estimate=pl.CostEstimate(flops=4 * 10**9, bytes_accessed=4 * 10**6, transcendentals=0),
    )(place, probes, words, *halo, *constants)


PAD = 3 * WIN


def gather_kernel(place_ref, pos_ref, *refs):
    out_hbm, window, out_buf, sems = refs[8:]
    side, core, row_base = place_ref[0], place_ref[1], place_ref[2]

    def copy(group):
        rows = pl.ds(pl.multiple_of(8 * group, 8), 8)
        return pltpu.make_async_copy(out_buf.at[rows], out_hbm.at[rows], sems.at[group])

    def step(group, carry):
        for par in range(2):
            parity = core if par == 0 else 1 - core
            for i in range(4):
                k = 4 * group + i
                row = pos_ref[0, 2 * k + parity] - row_base
                start = jnp.where(row < GROUP, row, jnp.where(row > 2 * GROUP, row - GROUP, GROUP))
                base = (2 * i + parity) * PAD + WIN - start
                places = (GROUP + GROUP * side, 2 * GROUP - GROUP * side, 3 * GROUP * (1 - side), 3 * GROUP * side)
                for piece, at in zip(refs[4 * par : 4 * par + 4], places):
                    window[pl.ds(base + at, GROUP), :] = piece[k].astype(jnp.float32)
        rows = pl.ds(pl.multiple_of(8 * group, 8), 8)
        for u in range(WIN):
            out_buf[rows, u * WIN : (u + 1) * WIN] = window[pl.ds(WIN + u, 8, stride=PAD), :]
        copy(group).start()
        return carry

    groups = out_buf.shape[0] // 8
    lax.fori_loop(0, groups, step, 0)
    for group in range(groups):
        copy(group).wait()


def put_together(place, positions, pieces):
    probes = positions.shape[1]
    smem = pl.BlockSpec(memory_space=pltpu.SMEM)
    vmem = pl.BlockSpec(memory_space=pltpu.VMEM)
    return pl.pallas_call(
        gather_kernel,
        out_shape=jax.ShapeDtypeStruct((probes, WIN * WIN), jnp.float32),
        in_specs=[smem, smem] + [vmem] * 8,
        out_specs=pl.BlockSpec(memory_space=pltpu.HBM),
        scratch_shapes=[
            pltpu.VMEM((8 * PAD, LANES), jnp.float32),
            pltpu.VMEM((probes, WIN * WIN), jnp.float32),
            pltpu.SemaphoreType.DMA((probes // 8,)),
        ],
        compiler_params=pltpu.CompilerParams(vmem_limit_bytes=16 * MIB),
    )(place, positions, *pieces)


def local(atoms, phases, aperture, tilts, positions):
    rows_here, width = atoms.shape[1], atoms.shape[2]
    probes = positions.shape[0]
    positions = positions.T
    strip, beam = lax.axis_index("strip"), lax.axis_index("beam")
    strips, ways = lax.axis_size("strip"), lax.axis_size("beam")
    rows_total = rows_here * strips
    beams = tilts.shape[0] * ways
    cores = CORES
    side, core = beam // cores, beam % cores
    near_strip = jnp.where(side == 0, strip - 1 + strips, strip + 1) % strips
    near_base = near_strip * rows_here + jnp.where(side == 0, rows_here, -rows_here)
    place = jnp.stack([side, core, strip * rows_here, near_base]).astype(jnp.int32)

    def across(array, dest):
        pairs = []
        for s in range(strips):
            for b in range(ways):
                to_s, to_b = dest(s, b // cores, b % cores)
                pairs.append((b * strips + s, (to_b[0] * cores + to_b[1]) * strips + to_s % strips))
        return lax.ppermute(array, ("beam", "strip"), pairs)

    def swap_cores(array):
        return across(array, lambda s, y, c: (s, (y, 1 - c)))

    packed = pack_rows(atoms, positions)
    mine = across(packed, lambda s, y, c: (s + 1 - 2 * y, (y, c)))
    packed, tilts, aperture = lax.optimization_barrier((packed, tilts, aperture))
    beam_rows = jnp.concatenate([tilts.astype(jnp.float32), aperture[:, None]], axis=1)
    beam_rows = [
        beam_rows,
        swap_cores(beam_rows),
        across(beam_rows, lambda s, y, c: (s, (1 - y, c))),
        across(beam_rows, lambda s, y, c: (s, (1 - y, 1 - c))),
    ]
    beam_rows = jnp.concatenate(beam_rows, axis=0)
    words = own_words(place, atoms)
    table = probe_table(beam_rows, phases, rows_total, width)
    mine, words, table = lax.optimization_barrier((mine, words, table))
    near = mine[:2, width // cores : width // cores + probes].astype(jnp.int32)
    ext, words = propagate(beams, place, near, words, [mine, swap_cores(mine)], table)
    far = across(ext, lambda s, y, c: (s - 1 + 2 * y, (1 - y, c)))
    own = propagate(beams, place, positions, words, [], table)
    own, far, ext = lax.optimization_barrier((own, far, ext))
    facing = across(own, lambda s, y, c: (s, (1 - y, c)))
    same = across(ext, lambda s, y, c: (s - 1 + 2 * y, (y, c)))
    pieces = [own, facing, same, far]
    return put_together(place, positions, pieces + [swap_cores(piece) for piece in pieces])


def solution(mesh):
    in_specs = (P(None, "strip", None), P(), P("beam"), P("beam", None), P("strip", None))
    out_specs = P("strip", None)
    return jax.shard_map(local, mesh=mesh, in_specs=in_specs, out_specs=out_specs, check_vma=False)
```

```python
import math

import jax
import jax.numpy as jnp
import ml_dtypes
import numpy as np
from jax import lax
from jax.experimental import pallas as pl
from jax.experimental.pallas import tpu as pltpu
from jax.sharding import PartitionSpec as P

HALFW = 32
TYPES = 4
WIN = 128
LANES = 128
GROUP = 64
PACK = 32
GROUPS = 6
BITS = 4
HALO0 = 64
HALO1 = 32
HALO = HALO0 + HALO1
TABLE = 384
MIB = 1024 * 1024
CORES = 2


def taps(offset):
    steps = np.arange(-HALFW, HALFW + 1, dtype=np.float32)
    weights = 1.0 - 0.5 * (steps / (HALFW + 1.0)) ** 2
    scale = np.sqrt(np.sum(weights * weights))
    offset = offset.astype(np.float32)
    weight = (1.0 - 0.5 * (offset / (HALFW + 1.0)) ** 2) / scale
    chirp = np.float32(math.pi) * offset * offset / np.float32(2.0 * HALFW + 1.0)
    inside = np.abs(offset) <= HALFW
    real = np.where(inside, np.cos(chirp) * weight, 0.0)
    imag = np.where(inside, np.sin(chirp) * weight, 0.0)
    return real.astype(np.float32), imag.astype(np.float32)


def x_matrix(sources, targets):
    rows = []
    for start in range(0, len(sources), LANES):
        src = sources[start : start + LANES]
        real, imag = taps(targets[None, :] - src[:, None] + HALFW)
        rows.append(np.concatenate([real, imag], axis=1))
        rows.append(np.concatenate([-imag, real], axis=1))
    return np.concatenate(rows, axis=0).astype(ml_dtypes.bfloat16)


def y_matrix():
    out = np.arange(GROUP)[:, None]
    src = np.arange(2 * GROUP)[None, :]
    real, imag = taps(out - src + HALFW)
    upper = np.concatenate([real, -imag], axis=1)
    lower = np.concatenate([imag, real], axis=1)
    return np.concatenate([upper, lower], axis=0).astype(ml_dtypes.bfloat16)


def matrices():
    first = x_matrix(np.arange(2 * LANES), np.arange(LANES))
    second = x_matrix(np.arange(LANES, 2 * LANES), np.arange(LANES, 2 * LANES))
    second = second.reshape(2 * LANES, 2, LANES)
    second[:, :, LANES // 2 :] = 0
    return first, second.reshape(2 * LANES, 2 * LANES), y_matrix()


def pack_kernel(atoms_hbm, pos_ref, out_ref, zero_buf, one_buf, pos_buf, sems):
    half = zero_buf.shape[1]
    rows = atoms_hbm.shape[1]
    beam = lax.axis_index("beam")
    side, core = beam // CORES, beam % CORES
    parts = sems.shape[0] // 2
    step = half // parts
    copies = []
    for layer, buf in ((0, zero_buf), (1, one_buf)):
        depth = buf.shape[0]
        top = pl.multiple_of((1 - side) * (rows - depth), depth)
        for part in range(parts):
            left = pl.multiple_of(core * half + part * step, LANES)
            copies.append(
                pltpu.make_async_copy(
                    atoms_hbm.at[layer, pl.ds(top, depth), pl.ds(left, step)],
                    buf.at[:, pl.ds(part * step, step)],
                    sems.at[parts * layer + part],
                )
            )
    for copy in copies:
        copy.start()
    pos_buf[...] = jnp.zeros(pos_buf.shape, jnp.int32)
    pos_buf[:2, : pos_ref.shape[1]] = pos_ref[...]
    out_ref[half // LANES * HALO :, :] = pos_buf[...].astype(jnp.int16)
    for layer, (buf, first) in enumerate(((zero_buf, 0), (one_buf, HALO0))):
        for part in range(parts):
            copies[parts * layer + part].wait()
            for tile in range(part * step // LANES, (part + 1) * step // LANES):
                rows = slice(tile * HALO + first, tile * HALO + first + buf.shape[0])
                out_ref[rows, :] = buf[:, tile * LANES : (tile + 1) * LANES].astype(jnp.int16)


def pack_rows(atoms, positions):
    half = atoms.shape[2] // CORES
    vmem = pl.BlockSpec(memory_space=pltpu.VMEM)
    return pl.pallas_call(
        pack_kernel,
        out_shape=pltpu.VMEM((half // LANES * HALO + 16, LANES), jnp.int16),
        in_specs=[pl.BlockSpec(memory_space=pltpu.HBM), vmem],
        out_specs=vmem,
        scratch_shapes=[
            pltpu.VMEM((HALO0, half), jnp.int32),
            pltpu.VMEM((HALO1, half), jnp.int32),
            pltpu.VMEM((16, LANES), jnp.int32),
            pltpu.SemaphoreType.DMA((4,)),
        ],
        compiler_params=pltpu.CompilerParams(vmem_limit_bytes=60 * MIB),
    )(atoms, positions)


def words_kernel(place_ref, atoms_hbm, out_ref, buf, sems):
    upper = place_ref[0] == 1
    parts = sems.shape[0]
    step = buf.shape[2] // parts
    copies = [
        pltpu.make_async_copy(
            atoms_hbm.at[:, :, pl.ds(k * step, step)], buf.at[:, :, pl.ds(k * step, step)], sems.at[k]
        )
        for k in range(parts)
    ]
    for copy in copies:
        copy.start()
    depth = out_ref.shape[1]
    for k in range(parts):
        copies[k].wait()
        for tile in range(k * step // LANES, (k + 1) * step // LANES):
            at = slice(tile * LANES, (tile + 1) * LANES)
            code = buf[0, :, at] + TYPES * buf[1, :, at]
            blocks = [code[n * PACK : (n + 1) * PACK] for n in range(buf.shape[1] // PACK)]
            halo = HALO0 // PACK
            for w in range(depth // PACK):
                words = []
                for first in (halo, 0):
                    word = None
                    for g in range(GROUPS):
                        block = w + g - first
                        if 0 <= block < len(blocks):
                            term = blocks[block] << (BITS * g)
                            word = term if word is None else word | term
                    words.append(word)
                out_ref[tile, w * PACK : (w + 1) * PACK, :] = jnp.where(upper, words[1], words[0])


def own_words(place, atoms):
    width = atoms.shape[2]
    return pl.pallas_call(
        words_kernel,
        out_shape=pltpu.VMEM((width // LANES, GROUP + PACK, LANES), jnp.int32),
        in_specs=[pl.BlockSpec(memory_space=pltpu.SMEM), pl.BlockSpec(memory_space=pltpu.HBM)],
        out_specs=pl.BlockSpec(memory_space=pltpu.VMEM),
        scratch_shapes=[pltpu.VMEM(atoms.shape, jnp.int32), pltpu.SemaphoreType.DMA((8,))],
        compiler_params=pltpu.CompilerParams(vmem_limit_bytes=60 * MIB),
        cost_estimate=pl.CostEstimate(flops=20 * atoms.size, bytes_accessed=6 * atoms.size, transcendentals=0),
    )(place, atoms)


def cos_turns(turns):
    angle = (2.0 * math.pi) * (0.25 - jnp.abs(turns - jnp.round(turns)))
    square = angle * angle
    total = jnp.full_like(square, 1.0)
    for k in (12, 10, 8, 6, 4, 2):
        total = 1.0 - square * total * (1.0 / (k * (k + 1)))
    return angle * total


def probe_kernel(rows_total, width, beam_ref, phase_ref, *refs):
    matrices_hbm, (out_ref, values_ref), matrices_ref, sems = refs[:3], refs[3:5], refs[5:8], refs[8]
    copies = [pltpu.make_async_copy(a, b, sems.at[n]) for n, (a, b) in enumerate(zip(matrices_hbm, matrices_ref))]
    for copy in copies:
        copy.start()
    beams = beam_ref.shape[0]
    precise = lax.Precision.HIGHEST
    lane = lax.broadcasted_iota(jnp.int32, (1, LANES), 1)
    tilt_y = jnp.zeros((1, LANES), jnp.float32)
    for beam in range(beams):
        tilt_y = jnp.where(lane % beams == beam, beam_ref[beam, 1], tilt_y)
    quarter = jnp.where(lane < beams, 0.0, 0.25)
    row = lax.broadcasted_iota(jnp.int32, (TABLE, LANES), 0) - TABLE // 2
    along_y = cos_turns(row.astype(jnp.float32) * tilt_y / rows_total - quarter)
    along_y = jnp.where(lane < 2 * beams, along_y, 0.0)

    sub = lax.broadcasted_iota(jnp.int32, (2 * beams, 1), 0)
    tilt_x = jnp.zeros((2 * beams, 1), jnp.float32)
    weight = jnp.zeros((2 * beams, 1), jnp.float32)
    for beam in range(beams):
        tilt_x = jnp.where(sub % beams == beam, beam_ref[beam, 0], tilt_x)
        weight = jnp.where(sub % beams == beam, beam_ref[beam, 2], weight)
    col = lax.broadcasted_iota(jnp.int32, (2 * beams, 2 * LANES), 1) - LANES
    turns = col.astype(jnp.float32) * tilt_x / width
    shift = jnp.where(sub < beams, 0.0, 0.25)
    right_re = weight * cos_turns(turns + shift)
    right_im = weight * cos_turns(turns + shift - 0.25)
    right = jnp.concatenate([right_re, right_im], axis=1)
    right = jnp.concatenate([right, jnp.zeros((LANES - 2 * beams, 4 * LANES), jnp.float32)], axis=0)
    table = jnp.dot(along_y, right, precision=precise, preferred_element_type=jnp.float32)
    for part in range(2):
        for tile in range(2):
            lo = (2 * part + tile) * LANES
            out_ref[part, tile] = table[:, lo : lo + LANES]

    sub = lax.broadcasted_iota(jnp.int32, (4 * TYPES, LANES), 0)
    angle = jnp.zeros((4 * TYPES, LANES), jnp.float32)
    for layer in range(2):
        for kind in range(TYPES):
            mine = (sub // (2 * TYPES) == layer) & (sub % TYPES == kind)
            angle = jnp.where(mine, phase_ref[layer, kind], angle)
    quarter = jnp.where((sub // TYPES) % 2 == 0, 0.0, 0.25)
    values_ref[...] = cos_turns(angle * (0.5 / math.pi) - quarter)
    for copy in copies:
        copy.wait()


def probe_table(beam_rows, phases, rows_total, width):
    bands = matrices()

    def kernel(*refs):
        probe_kernel(rows_total, width, *refs)

    smem = pl.BlockSpec(memory_space=pltpu.SMEM)
    vmem = pl.BlockSpec(memory_space=pltpu.VMEM)
    return pl.pallas_call(
        kernel,
        out_shape=[pltpu.VMEM((2, 2, TABLE, LANES), jnp.float32), pltpu.VMEM((4 * TYPES, LANES), jnp.float32)]
        + [pltpu.VMEM(matrix.shape, jnp.bfloat16) for matrix in bands],
        in_specs=[smem, smem] + [pl.BlockSpec(memory_space=pltpu.HBM)] * 3,
        out_specs=[vmem] * 5,
        scratch_shapes=[pltpu.SemaphoreType.DMA((3,))],
        compiler_params=pltpu.CompilerParams(vmem_limit_bytes=60 * MIB),
        cost_estimate=pl.CostEstimate(flops=10**8, bytes_accessed=10**6, transcendentals=10**5),
    )(beam_rows, phases, *bands)


def merge_rows(side, core, halo_refs, words_in, words):
    half_tiles = words.shape[0] // CORES

    depth = words.shape[1]

    def merge(upper):
        top = PACK * GROUPS + GROUP - HALO0 if upper else 0
        lo = 0 if upper else HALO0 - HALO1
        for source, at in zip(halo_refs, (core, 1 - core)):
            for tile in range(half_tiles):
                zero = source[tile * HALO : tile * HALO + HALO0, :].astype(jnp.int32)
                one = source[tile * HALO + HALO0 : (tile + 1) * HALO, :].astype(jnp.int32) * TYPES
                blocks = [zero[:PACK], zero[PACK:]]
                blocks[lo // PACK] = blocks[lo // PACK] + one
                index = at * half_tiles + tile
                for w in range(depth // PACK):
                    word = None
                    for g in range(GROUPS):
                        block = w + g - top // PACK
                        if 0 <= block < 2:
                            term = blocks[block] << (BITS * g)
                            word = term if word is None else word | term
                    if word is not None:
                        rows = slice(w * PACK, (w + 1) * PACK)
                        words[index, rows, :] = words_in[index, rows, :] | word

    @pl.when(side == 0)
    def _():
        merge(False)

    @pl.when(side == 1)
    def _():
        merge(True)


def run_tasks(beams, batch_size, side, total, words, table_ref, values_ref, first_ref, second_ref, ymat_ref, result, scratch):
    left, crossed, right, codes_new, codes_old, row_list, col_list, slot_list = scratch
    tiles = words.shape[0]
    f32, bf16, i16 = jnp.float32, jnp.bfloat16, jnp.int16

    def values(layer):
        rows = [values_ref[2 * TYPES * layer + k : 2 * TYPES * layer + k + 1, :].astype(bf16) for k in range(2 * TYPES)]
        return rows[:TYPES], rows[TYPES:]

    cos0, sin0 = values(0)
    cos1, sin1 = values(1)
    lane = lax.broadcasted_iota(jnp.int32, (1, LANES), 1)

    def transmission(code, bit, cos_v, sin_v):
        b0 = (code & i16(1 << bit)) != 0
        b1 = (code & i16(2 << bit if bit < 14 else -(1 << 15))) != 0
        out = []
        for v in (cos_v, sin_v):
            spread = [jnp.broadcast_to(value, code.shape) for value in v]
            out.append(jnp.where(b1, jnp.where(b0, spread[3], spread[2]), jnp.where(b0, spread[1], spread[0])))
        return out

    def split(word):
        return word.astype(i16), (word >> 16).astype(i16)

    def tile_cols(j, part):
        return slice((2 * j + part) * LANES, (2 * j + part + 1) * LANES)

    def waves(batch):
        for k in range(batch_size):
            at = jnp.minimum(batch_size * batch + k, total - 1)
            row, col = row_list[at], col_list[at]
            start = jnp.clip(row - GROUP, 0, GROUP)
            delta = start - GROUP * (1 - side) - row + TABLE // 2
            tile0 = col // LANES + tiles - 1
            shift = lax.rem(col, LANES)
            back = lax.rem(LANES - shift, LANES)
            rolled = []
            for j in range(3):
                word = words[lax.rem(tile0 + j, tiles), pl.ds(start, PACK), :]
                rolled.append(pltpu.roll(word, back, 1))
            keep = lane < LANES - shift
            window = [jnp.where(keep, rolled[j], rolled[j + 1]) for j in range(2)]
            turned = [pltpu.roll(w, LANES - HALFW, 1) for w in window]
            inner = [jnp.where(lane < LANES - HALFW, turned[0], turned[1]), turned[1]]
            for j in range(2):
                codes_new[k, j, 0], codes_new[k, j, 1] = split(inner[j])
                codes = split(window[j])
                for g in range(GROUPS):
                    t_re, t_im = transmission(codes[g // 4], BITS * (g % 4), cos0, sin0)
                    p_re = table_ref[0, j, pl.ds(delta + g * PACK, PACK), :].astype(bf16)
                    p_im = table_ref[1, j, pl.ds(delta + g * PACK, PACK), :].astype(bf16)
                    rows = slice(k * 3 * GROUP + g * PACK, k * 3 * GROUP + (g + 1) * PACK)
                    left[rows, tile_cols(j, 0)] = p_re * t_re - p_im * t_im
                    left[rows, tile_cols(j, 1)] = p_re * t_im + p_im * t_re
        for k in range(batch_size):
            rows = slice(k * 3 * GROUP, (k + 1) * 3 * GROUP)
            one = jnp.dot(left[rows, :], first_ref[...], preferred_element_type=f32).astype(bf16)
            two = jnp.dot(left[rows, 2 * LANES :], second_ref[...], preferred_element_type=f32).astype(bf16)
            for part in range(2):
                cols = slice(part * LANES, (part + 1) * LANES)
                crossed[k, part, :, :LANES] = one[:, cols]
                crossed[k, part, :, LANES:] = two[:, cols]

    def stack(k, b):
        rows = slice(b * GROUP, b * GROUP + 2 * GROUP)
        return jnp.concatenate([crossed[k, part, rows] for part in range(2)], axis=0)

    def rest(batch):
        for k in range(batch_size):
            for b in range(2):
                down = jnp.dot(ymat_ref[...], stack(k, b), preferred_element_type=f32)
                for j in range(2):
                    cols = slice(j * LANES, (j + 1) * LANES)
                    for part in range(2):
                        group = 2 * b + part + 1
                        t_re, t_im = transmission(codes_old[k, j, group // 4], BITS * (group % 4) + 2, cos1, sin1)
                        d_re = down[part * PACK : (part + 1) * PACK, cols].astype(bf16)
                        d_im = down[GROUP + part * PACK : GROUP + (part + 1) * PACK, cols].astype(bf16)
                        top = (2 * k + b) * GROUP + part * PACK
                        right[top : top + PACK, tile_cols(j, 0)] = d_re * t_re - d_im * t_im
                        right[top : top + PACK, tile_cols(j, 1)] = d_re * t_im + d_im * t_re
        one = jnp.dot(right[...], first_ref[...], preferred_element_type=f32).astype(bf16)
        stacks = []
        for k in range(batch_size):
            rows = slice(2 * k * GROUP, (2 * k + 2) * GROUP)
            stacks.append(jnp.concatenate([one[rows, :LANES], one[rows, LANES:]], axis=0))
        exit_waves = jnp.dot(ymat_ref[...], jnp.concatenate(stacks, axis=1), preferred_element_type=f32)
        exit_waves = exit_waves.astype(bf16).astype(f32)
        for k in range(batch_size):
            cols = slice(k * LANES, (k + 1) * LANES)
            re, im = exit_waves[:GROUP, cols], exit_waves[GROUP:, cols]
            slot = slot_list[jnp.minimum(batch_size * batch + k, total - 1)]
            result[slot] = ((re * re + im * im) * (1.0 / beams)).astype(bf16)

    def step(batch, carry):
        rest(batch - 1)
        waves(batch)
        codes_old[...] = codes_new[...]
        return carry

    batches = (total + batch_size - 1) // batch_size
    waves(0)
    codes_old[...] = codes_new[...]
    lax.fori_loop(1, batches, step, 0)
    rest(batches - 1)


def ext_kernel(beams, batch_size, place_ref, near_ref, words_in, mine_ref, other_ref, *refs):
    constants, (low_ref, high_ref, words), out_ref, scratch = refs[:5], refs[5:8], refs[8], refs[9:]
    row_list, col_list, slot_list = scratch[5:]
    side, core, near_base = place_ref[0], place_ref[1], place_ref[3]
    merge_rows(side, core, (mine_ref, other_ref), words_in, words)

    def add(k, found):
        probe = CORES * k + core
        row = near_ref[0, probe] - near_base
        reaches = jnp.where(side == 0, row > -GROUP, row < 4 * GROUP)
        row_list[found] = row
        col_list[found] = near_ref[1, probe]
        slot_list[found] = k
        return found + reaches.astype(jnp.int32)

    total = lax.fori_loop(0, out_ref.shape[0], add, 0, unroll=True)

    @pl.when(total > 0)
    def _():
        run_tasks(beams, batch_size, side, total, words, *constants, out_ref, scratch)

    half = low_ref.shape[0]
    low_ref[...] = out_ref[:half]
    high_ref[...] = out_ref[half:]


def own_kernel(beams, batch_size, place_ref, pos_ref, words, *refs):
    constants, (low_ref, high_ref), out_ref, scratch = refs[:5], refs[5:7], refs[7], refs[8:]
    row_list, col_list, slot_list = scratch[5:]
    side, core, row_base = place_ref[0], place_ref[1], place_ref[2]
    count = out_ref.shape[0]

    def add(k, carry):
        probe = CORES * k + core
        row_list[k] = pos_ref[0, probe] - row_base
        col_list[k] = pos_ref[1, probe]
        slot_list[k] = k
        return carry

    lax.fori_loop(0, count, add, 0, unroll=True)
    run_tasks(beams, batch_size, side, count, words, *constants, out_ref, scratch)
    low_ref[...] = out_ref[: count // 2]
    high_ref[...] = out_ref[count // 2 :]


def propagate(beams, place, probes, words, halo, constants):
    count = probes.shape[1] // CORES
    smem = pl.BlockSpec(memory_space=pltpu.SMEM)
    vmem = pl.BlockSpec(memory_space=pltpu.VMEM)
    ext = bool(halo)
    body = ext_kernel if ext else own_kernel
    batch_size = 10 if ext else count

    def kernel(*refs):
        body(beams, batch_size, *refs)

    half = jax.ShapeDtypeStruct((count // 2, GROUP, WIN), jnp.bfloat16)
    return pl.pallas_call(
        kernel,
        out_shape=[half, half, pltpu.VMEM(words.shape, jnp.int32)] if ext else [half, half],
        in_specs=[smem] * 2 + [vmem] * (8 if ext else 6),
        out_specs=[vmem] * (3 if ext else 2),
        input_output_aliases={2: 2} if ext else {},
        scratch_shapes=[
            pltpu.VMEM((count, GROUP, WIN), jnp.bfloat16),
            pltpu.VMEM((batch_size * 3 * GROUP, 4 * LANES), jnp.bfloat16),
            pltpu.VMEM((batch_size, 2, 3 * GROUP, 2 * LANES), jnp.bfloat16),
            pltpu.VMEM((batch_size * 2 * GROUP, 4 * LANES), jnp.bfloat16),
            pltpu.VMEM((batch_size, 2, 2, PACK, LANES), jnp.int16),
            pltpu.VMEM((batch_size, 2, 2, PACK, LANES), jnp.int16),
            pltpu.SMEM((count + 1,), jnp.int32),
            pltpu.SMEM((count + 1,), jnp.int32),
            pltpu.SMEM((count + 1,), jnp.int32),
        ],
        compiler_params=pltpu.CompilerParams(vmem_limit_bytes=40 * MIB),
        cost_estimate=pl.CostEstimate(flops=4 * 10**9, bytes_accessed=4 * 10**6, transcendentals=0),
    )(place, probes, words, *halo, *constants)


def merge_kernel(half, place_ref, pos_ref, own_ref, same_ref, out_ref):
    side, core, row_base = place_ref[0], place_ref[1], place_ref[2]
    line = lax.broadcasted_iota(jnp.int32, (GROUP, LANES), 0).astype(jnp.int16)
    for k in range(out_ref.shape[0]):
        row = pos_ref[0, CORES * (k + half * out_ref.shape[0]) + core] - row_base
        low = jnp.where(side == 0, jnp.clip(row - 2 * GROUP, 0, GROUP), 0)
        high = jnp.where(side == 0, GROUP, jnp.clip(row, 0, GROUP))
        kept = (line >= low.astype(jnp.int16)) & (line < high.astype(jnp.int16))
        out_ref[k] = jnp.where(kept, own_ref[k], same_ref[k])


def merge_pieces(half, place, positions, own, same):
    def kernel(*refs):
        merge_kernel(half, *refs)

    smem = pl.BlockSpec(memory_space=pltpu.SMEM)
    vmem = pl.BlockSpec(memory_space=pltpu.VMEM)
    return pl.pallas_call(
        kernel,
        out_shape=jax.ShapeDtypeStruct(own.shape, own.dtype),
        in_specs=[smem, smem, vmem, vmem],
        out_specs=vmem,
        compiler_params=pltpu.CompilerParams(vmem_limit_bytes=16 * MIB),
    )(place, positions, own, same)


PAD = 3 * WIN + 1


def gather_kernel(place_ref, pos_ref, *refs):
    out_hbm, window, out_buf, sems = refs[8:]
    side, core, row_base = place_ref[0], place_ref[1], place_ref[2]

    def copy(group):
        rows = pl.ds(pl.multiple_of(8 * group, 8), 8)
        return pltpu.make_async_copy(out_buf.at[rows], out_hbm.at[rows], sems.at[group])

    def step(half, local, carry):
        group = local + half * groups // 2
        for par in range(2):
            parity = core if par == 0 else 1 - core
            own, facing = refs[4 * par + half], refs[4 * par + 2 + half]
            for i in range(4):
                row = pos_ref[0, 2 * (4 * group + i) + parity] - row_base
                k = 4 * local + i
                below = row > 2 * GROUP
                start = jnp.where(row < GROUP, row, jnp.where(below, row - GROUP, GROUP))
                base = (2 * i + parity) * PAD + WIN - start
                mine, across = own[k].astype(jnp.float32), facing[k].astype(jnp.float32)
                window[pl.ds(base + GROUP + GROUP * side, GROUP), :] = mine
                window[pl.ds(base + 2 * GROUP - GROUP * side, GROUP), :] = across
                wrapped = jnp.where(below == (side == 0), mine, across)
                window[pl.ds(base + jnp.where(below, 3 * GROUP, 0), GROUP), :] = wrapped
        rows = pl.ds(pl.multiple_of(8 * group, 8), 8)
        for u in range(WIN):
            out_buf[rows, u * WIN : (u + 1) * WIN] = window[pl.ds(WIN + u, 8, stride=PAD), :]
        copy(group).start()
        return carry

    groups = out_buf.shape[0] // 8
    for half in range(2):
        lax.fori_loop(0, groups // 2, lambda local, carry, half=half: step(half, local, carry), 0)
    for group in range(groups):
        copy(group).wait()


def put_together(place, positions, pieces):
    probes = positions.shape[1]
    smem = pl.BlockSpec(memory_space=pltpu.SMEM)
    vmem = pl.BlockSpec(memory_space=pltpu.VMEM)
    return pl.pallas_call(
        gather_kernel,
        out_shape=jax.ShapeDtypeStruct((probes, WIN * WIN), jnp.float32),
        in_specs=[smem, smem] + [vmem] * 8,
        out_specs=pl.BlockSpec(memory_space=pltpu.HBM),
        scratch_shapes=[
            pltpu.VMEM((8 * PAD, LANES), jnp.float32),
            pltpu.VMEM((probes, WIN * WIN), jnp.float32),
            pltpu.SemaphoreType.DMA((probes // 8,)),
        ],
        compiler_params=pltpu.CompilerParams(vmem_limit_bytes=16 * MIB),
    )(place, positions, *pieces)


def local(atoms, phases, aperture, tilts, positions):
    rows_here, width = atoms.shape[1], atoms.shape[2]
    probes = positions.shape[0]
    positions = positions.T
    strip, beam = lax.axis_index("strip"), lax.axis_index("beam")
    strips, ways = lax.axis_size("strip"), lax.axis_size("beam")
    rows_total = rows_here * strips
    beams = tilts.shape[0] * ways
    cores = CORES
    side, core = beam // cores, beam % cores
    near_strip = jnp.where(side == 0, strip - 1 + strips, strip + 1) % strips
    near_base = near_strip * rows_here + jnp.where(side == 0, rows_here, -rows_here)
    place = jnp.stack([side, core, strip * rows_here, near_base]).astype(jnp.int32)

    def across(array, dest):
        pairs = []
        for s in range(strips):
            for b in range(ways):
                to_s, to_b = dest(s, b // cores, b % cores)
                pairs.append((b * strips + s, (to_b[0] * cores + to_b[1]) * strips + to_s % strips))
        return lax.ppermute(array, ("beam", "strip"), pairs)

    def swap_cores(array):
        return across(array, lambda s, y, c: (s, (y, 1 - c)))

    packed = pack_rows(atoms, positions)
    mine = across(packed, lambda s, y, c: (s + 1 - 2 * y, (y, c)))
    packed, tilts, aperture = lax.optimization_barrier((packed, tilts, aperture))
    beam_rows = jnp.concatenate([tilts.astype(jnp.float32), aperture[:, None]], axis=1)
    beam_rows = [
        beam_rows,
        swap_cores(beam_rows),
        across(beam_rows, lambda s, y, c: (s, (1 - y, c))),
        across(beam_rows, lambda s, y, c: (s, (1 - y, 1 - c))),
    ]
    beam_rows = jnp.concatenate(beam_rows, axis=0)
    words = own_words(place, atoms)
    table = probe_table(beam_rows, phases, rows_total, width)
    mine, words, table = lax.optimization_barrier((mine, words, table))
    near = mine[width // cores // LANES * HALO :][:2, :probes].astype(jnp.int32)
    *ext, words = propagate(beams, place, near, words, [mine, swap_cores(mine)], table)
    same = [across(half, lambda s, y, c: (s - 1 + 2 * y, (y, c))) for half in ext]
    own = propagate(beams, place, positions, words, [], table)
    own = [merge_pieces(n, place, positions, *pair) for n, pair in enumerate(zip(own, same))]
    facing = [across(half, lambda s, y, c: (s, (1 - y, c))) for half in own]
    pieces = own + facing
    return put_together(place, positions, pieces + [swap_cores(piece) for piece in pieces])


def solution(mesh):
    in_specs = (P(None, "strip", None), P(), P("beam"), P("beam", None), P("strip", None))
    out_specs = P("strip", None)
    return jax.shard_map(local, mesh=mesh, in_specs=in_specs, out_specs=out_specs, check_vma=False)
```

```python
import math

import jax
import jax.numpy as jnp
import ml_dtypes
import numpy as np
from jax import lax
from jax.experimental import pallas as pl
from jax.experimental.pallas import tpu as pltpu
from jax.sharding import PartitionSpec as P

HALFW = 32
TYPES = 4
WIN = 128
LANES = 128
GROUP = 64
PACK = 32
GROUPS = 6
BITS = 4
HALO0 = 64
HALO1 = 32
HALO = HALO0 + HALO1
TABLE = 384
MIB = 1024 * 1024
CORES = 2


def taps(offset):
    steps = np.arange(-HALFW, HALFW + 1, dtype=np.float32)
    weights = 1.0 - 0.5 * (steps / (HALFW + 1.0)) ** 2
    scale = np.sqrt(np.sum(weights * weights))
    offset = offset.astype(np.float32)
    weight = (1.0 - 0.5 * (offset / (HALFW + 1.0)) ** 2) / scale
    chirp = np.float32(math.pi) * offset * offset / np.float32(2.0 * HALFW + 1.0)
    inside = np.abs(offset) <= HALFW
    real = np.where(inside, np.cos(chirp) * weight, 0.0)
    imag = np.where(inside, np.sin(chirp) * weight, 0.0)
    return real.astype(np.float32), imag.astype(np.float32)


def x_matrix(sources, targets):
    rows = []
    for start in range(0, len(sources), LANES):
        src = sources[start : start + LANES]
        real, imag = taps(targets[None, :] - src[:, None] + HALFW)
        rows.append(np.concatenate([real, imag], axis=1))
        rows.append(np.concatenate([-imag, real], axis=1))
    return np.concatenate(rows, axis=0).astype(ml_dtypes.bfloat16)


def y_matrix():
    out = np.arange(GROUP)[:, None]
    src = np.arange(2 * GROUP)[None, :]
    real, imag = taps(out - src + HALFW)
    upper = np.concatenate([real, -imag], axis=1)
    lower = np.concatenate([imag, real], axis=1)
    return np.concatenate([upper, lower], axis=0).astype(ml_dtypes.bfloat16)


def matrices():
    first = x_matrix(np.arange(2 * LANES), np.arange(LANES))
    second = x_matrix(np.arange(LANES, 2 * LANES), np.arange(LANES, 2 * LANES))
    second = second.reshape(2 * LANES, 2, LANES)
    second[:, :, LANES // 2 :] = 0
    return first, second.reshape(2 * LANES, 2 * LANES), y_matrix()


def pack_kernel(atoms_hbm, pos_ref, out_ref, zero_buf, one_buf, pos_buf, sems):
    half = zero_buf.shape[1]
    rows = atoms_hbm.shape[1]
    beam = lax.axis_index("beam")
    side, core = beam // CORES, beam % CORES
    parts = sems.shape[0] // 2
    step = half // parts
    copies = []
    for layer, buf in ((0, zero_buf), (1, one_buf)):
        depth = buf.shape[0]
        top = pl.multiple_of((1 - side) * (rows - depth), depth)
        for part in range(parts):
            left = pl.multiple_of(core * half + part * step, LANES)
            copies.append(
                pltpu.make_async_copy(
                    atoms_hbm.at[layer, pl.ds(top, depth), pl.ds(left, step)],
                    buf.at[:, pl.ds(part * step, step)],
                    sems.at[parts * layer + part],
                )
            )
    for copy in copies:
        copy.start()
    pos_buf[...] = jnp.zeros(pos_buf.shape, jnp.int32)
    pos_buf[:2, : pos_ref.shape[1]] = pos_ref[...]
    out_ref[half // LANES * HALO :, :] = pos_buf[...].astype(jnp.int16)
    for layer, (buf, first) in enumerate(((zero_buf, 0), (one_buf, HALO0))):
        for part in range(parts):
            copies[parts * layer + part].wait()
            for tile in range(part * step // LANES, (part + 1) * step // LANES):
                rows = slice(tile * HALO + first, tile * HALO + first + buf.shape[0])
                out_ref[rows, :] = buf[:, tile * LANES : (tile + 1) * LANES].astype(jnp.int16)


def pack_rows(atoms, positions):
    half = atoms.shape[2] // CORES
    vmem = pl.BlockSpec(memory_space=pltpu.VMEM)
    return pl.pallas_call(
        pack_kernel,
        out_shape=pltpu.VMEM((half // LANES * HALO + 16, LANES), jnp.int16),
        in_specs=[pl.BlockSpec(memory_space=pltpu.HBM), vmem],
        out_specs=vmem,
        scratch_shapes=[
            pltpu.VMEM((HALO0, half), jnp.int32),
            pltpu.VMEM((HALO1, half), jnp.int32),
            pltpu.VMEM((16, LANES), jnp.int32),
            pltpu.SemaphoreType.DMA((4,)),
        ],
        compiler_params=pltpu.CompilerParams(vmem_limit_bytes=60 * MIB),
    )(atoms, positions)


def words_kernel(place_ref, atoms_hbm, out_ref, buf, sems):
    upper = place_ref[0] == 1
    parts = sems.shape[0]
    step = buf.shape[2] // parts
    copies = [
        pltpu.make_async_copy(
            atoms_hbm.at[:, :, pl.ds(k * step, step)], buf.at[:, :, pl.ds(k * step, step)], sems.at[k]
        )
        for k in range(parts)
    ]
    for copy in copies:
        copy.start()
    depth = out_ref.shape[1]
    for k in range(parts):
        copies[k].wait()
        for tile in range(k * step // LANES, (k + 1) * step // LANES):
            at = slice(tile * LANES, (tile + 1) * LANES)
            code = buf[0, :, at] + TYPES * buf[1, :, at]
            blocks = [code[n * PACK : (n + 1) * PACK] for n in range(buf.shape[1] // PACK)]
            halo = HALO0 // PACK
            for w in range(depth // PACK):
                words = []
                for first in (halo, 0):
                    word = None
                    for g in range(GROUPS):
                        block = w + g - first
                        if 0 <= block < len(blocks):
                            term = blocks[block] << (BITS * g)
                            word = term if word is None else word | term
                    words.append(word)
                out_ref[tile, w * PACK : (w + 1) * PACK, :] = jnp.where(upper, words[1], words[0])


def own_words(place, atoms):
    width = atoms.shape[2]
    return pl.pallas_call(
        words_kernel,
        out_shape=pltpu.VMEM((width // LANES, GROUP + PACK, LANES), jnp.int32),
        in_specs=[pl.BlockSpec(memory_space=pltpu.SMEM), pl.BlockSpec(memory_space=pltpu.HBM)],
        out_specs=pl.BlockSpec(memory_space=pltpu.VMEM),
        scratch_shapes=[pltpu.VMEM(atoms.shape, jnp.int32), pltpu.SemaphoreType.DMA((8,))],
        compiler_params=pltpu.CompilerParams(vmem_limit_bytes=60 * MIB),
        cost_estimate=pl.CostEstimate(flops=20 * atoms.size, bytes_accessed=6 * atoms.size, transcendentals=0),
    )(place, atoms)


def cos_turns(turns):
    angle = (2.0 * math.pi) * (0.25 - jnp.abs(turns - jnp.round(turns)))
    square = angle * angle
    total = jnp.full_like(square, 1.0)
    for k in (12, 10, 8, 6, 4, 2):
        total = 1.0 - square * total * (1.0 / (k * (k + 1)))
    return angle * total


def probe_kernel(rows_total, width, beam_ref, phase_ref, *refs):
    matrices_hbm, (out_ref, values_ref), matrices_ref, sems = refs[:3], refs[3:5], refs[5:8], refs[8]
    copies = [pltpu.make_async_copy(a, b, sems.at[n]) for n, (a, b) in enumerate(zip(matrices_hbm, matrices_ref))]
    for copy in copies:
        copy.start()
    beams = beam_ref.shape[0]
    precise = lax.Precision.HIGHEST
    lane = lax.broadcasted_iota(jnp.int32, (1, LANES), 1)
    tilt_y = jnp.zeros((1, LANES), jnp.float32)
    for beam in range(beams):
        tilt_y = jnp.where(lane % beams == beam, beam_ref[beam, 1], tilt_y)
    quarter = jnp.where(lane < beams, 0.0, 0.25)
    row = lax.broadcasted_iota(jnp.int32, (TABLE, LANES), 0) - TABLE // 2
    along_y = cos_turns(row.astype(jnp.float32) * tilt_y / rows_total - quarter)
    along_y = jnp.where(lane < 2 * beams, along_y, 0.0)

    sub = lax.broadcasted_iota(jnp.int32, (2 * beams, 1), 0)
    tilt_x = jnp.zeros((2 * beams, 1), jnp.float32)
    weight = jnp.zeros((2 * beams, 1), jnp.float32)
    for beam in range(beams):
        tilt_x = jnp.where(sub % beams == beam, beam_ref[beam, 0], tilt_x)
        weight = jnp.where(sub % beams == beam, beam_ref[beam, 2], weight)
    col = lax.broadcasted_iota(jnp.int32, (2 * beams, 2 * LANES), 1) - LANES
    turns = col.astype(jnp.float32) * tilt_x / width
    shift = jnp.where(sub < beams, 0.0, 0.25)
    right_re = weight * cos_turns(turns + shift)
    right_im = weight * cos_turns(turns + shift - 0.25)
    right = jnp.concatenate([right_re, right_im], axis=1)
    right = jnp.concatenate([right, jnp.zeros((LANES - 2 * beams, 4 * LANES), jnp.float32)], axis=0)
    table = jnp.dot(along_y, right, precision=precise, preferred_element_type=jnp.float32)
    for part in range(2):
        for tile in range(2):
            lo = (2 * part + tile) * LANES
            out_ref[part, tile] = table[:, lo : lo + LANES]

    sub = lax.broadcasted_iota(jnp.int32, (4 * TYPES, LANES), 0)
    angle = jnp.zeros((4 * TYPES, LANES), jnp.float32)
    for layer in range(2):
        for kind in range(TYPES):
            mine = (sub // (2 * TYPES) == layer) & (sub % TYPES == kind)
            angle = jnp.where(mine, phase_ref[layer, kind], angle)
    quarter = jnp.where((sub // TYPES) % 2 == 0, 0.0, 0.25)
    values_ref[...] = cos_turns(angle * (0.5 / math.pi) - quarter)
    for copy in copies:
        copy.wait()


def probe_table(beam_rows, phases, rows_total, width):
    bands = matrices()

    def kernel(*refs):
        probe_kernel(rows_total, width, *refs)

    smem = pl.BlockSpec(memory_space=pltpu.SMEM)
    vmem = pl.BlockSpec(memory_space=pltpu.VMEM)
    return pl.pallas_call(
        kernel,
        out_shape=[pltpu.VMEM((2, 2, TABLE, LANES), jnp.float32), pltpu.VMEM((4 * TYPES, LANES), jnp.float32)]
        + [pltpu.VMEM(matrix.shape, jnp.bfloat16) for matrix in bands],
        in_specs=[smem, smem] + [pl.BlockSpec(memory_space=pltpu.HBM)] * 3,
        out_specs=[vmem] * 5,
        scratch_shapes=[pltpu.SemaphoreType.DMA((3,))],
        compiler_params=pltpu.CompilerParams(vmem_limit_bytes=60 * MIB),
        cost_estimate=pl.CostEstimate(flops=10**8, bytes_accessed=10**6, transcendentals=10**5),
    )(beam_rows, phases, *bands)


def merge_rows(side, core, halo_refs, words_in, words):
    half_tiles = words.shape[0] // CORES

    depth = words.shape[1]

    def merge(upper):
        top = PACK * GROUPS + GROUP - HALO0 if upper else 0
        lo = 0 if upper else HALO0 - HALO1
        for source, at in zip(halo_refs, (core, 1 - core)):
            for tile in range(half_tiles):
                zero = source[tile * HALO : tile * HALO + HALO0, :].astype(jnp.int32)
                one = source[tile * HALO + HALO0 : (tile + 1) * HALO, :].astype(jnp.int32) * TYPES
                blocks = [zero[:PACK], zero[PACK:]]
                blocks[lo // PACK] = blocks[lo // PACK] + one
                index = at * half_tiles + tile
                for w in range(depth // PACK):
                    word = None
                    for g in range(GROUPS):
                        block = w + g - top // PACK
                        if 0 <= block < 2:
                            term = blocks[block] << (BITS * g)
                            word = term if word is None else word | term
                    if word is not None:
                        rows = slice(w * PACK, (w + 1) * PACK)
                        words[index, rows, :] = words_in[index, rows, :] | word

    @pl.when(side == 0)
    def _():
        merge(False)

    @pl.when(side == 1)
    def _():
        merge(True)


def run_tasks(beams, batch_size, side, total, words, table_ref, values_ref, first_ref, second_ref, ymat_ref, result, scratch):
    left, crossed, right, codes_new, codes_old, row_list, col_list, slot_list = scratch
    tiles = words.shape[0]
    f32, bf16, i16 = jnp.float32, jnp.bfloat16, jnp.int16

    def values(layer):
        rows = [values_ref[2 * TYPES * layer + k : 2 * TYPES * layer + k + 1, :].astype(bf16) for k in range(2 * TYPES)]
        return rows[:TYPES], rows[TYPES:]

    cos0, sin0 = values(0)
    cos1, sin1 = values(1)
    lane = lax.broadcasted_iota(jnp.int32, (1, LANES), 1)

    def transmission(code, bit, cos_v, sin_v):
        b0 = (code & i16(1 << bit)) != 0
        b1 = (code & i16(2 << bit if bit < 14 else -(1 << 15))) != 0
        out = []
        for v in (cos_v, sin_v):
            spread = [jnp.broadcast_to(value, code.shape) for value in v]
            out.append(jnp.where(b1, jnp.where(b0, spread[3], spread[2]), jnp.where(b0, spread[1], spread[0])))
        return out

    def split(word):
        return word.astype(i16), (word >> 16).astype(i16)

    def tile_cols(j, part):
        return slice((2 * j + part) * LANES, (2 * j + part + 1) * LANES)

    def waves(batch):
        for k in range(batch_size):
            at = jnp.minimum(batch_size * batch + k, total - 1)
            row, col = row_list[at], col_list[at]
            start = jnp.clip(row - GROUP, 0, GROUP)
            delta = start - GROUP * (1 - side) - row + TABLE // 2
            tile0 = col // LANES + tiles - 1
            shift = lax.rem(col, LANES)
            back = lax.rem(LANES - shift, LANES)
            rolled = []
            for j in range(3):
                word = words[lax.rem(tile0 + j, tiles), pl.ds(start, PACK), :]
                rolled.append(pltpu.roll(word, back, 1))
            keep = lane < LANES - shift
            window = [jnp.where(keep, rolled[j], rolled[j + 1]) for j in range(2)]
            turned = [pltpu.roll(w, LANES - HALFW, 1) for w in window]
            inner = [jnp.where(lane < LANES - HALFW, turned[0], turned[1]), turned[1]]
            for j in range(2):
                codes_new[k, j, 0], codes_new[k, j, 1] = split(inner[j])
                codes = split(window[j])
                for g in range(GROUPS):
                    t_re, t_im = transmission(codes[g // 4], BITS * (g % 4), cos0, sin0)
                    p_re = table_ref[0, j, pl.ds(delta + g * PACK, PACK), :].astype(bf16)
                    p_im = table_ref[1, j, pl.ds(delta + g * PACK, PACK), :].astype(bf16)
                    rows = slice(k * 3 * GROUP + g * PACK, k * 3 * GROUP + (g + 1) * PACK)
                    left[rows, tile_cols(j, 0)] = p_re * t_re - p_im * t_im
                    left[rows, tile_cols(j, 1)] = p_re * t_im + p_im * t_re
        for k in range(batch_size):
            rows = slice(k * 3 * GROUP, (k + 1) * 3 * GROUP)
            one = jnp.dot(left[rows, :], first_ref[...], preferred_element_type=f32).astype(bf16)
            two = jnp.dot(left[rows, 2 * LANES :], second_ref[...], preferred_element_type=f32).astype(bf16)
            for part in range(2):
                cols = slice(part * LANES, (part + 1) * LANES)
                crossed[k, part, :, :LANES] = one[:, cols]
                crossed[k, part, :, LANES:] = two[:, cols]

    def stack(k, b):
        rows = slice(b * GROUP, b * GROUP + 2 * GROUP)
        return jnp.concatenate([crossed[k, part, rows] for part in range(2)], axis=0)

    def rest(batch):
        for k in range(batch_size):
            for b in range(2):
                down = jnp.dot(ymat_ref[...], stack(k, b), preferred_element_type=f32)
                for j in range(2):
                    cols = slice(j * LANES, (j + 1) * LANES)
                    for part in range(2):
                        group = 2 * b + part + 1
                        t_re, t_im = transmission(codes_old[k, j, group // 4], BITS * (group % 4) + 2, cos1, sin1)
                        d_re = down[part * PACK : (part + 1) * PACK, cols].astype(bf16)
                        d_im = down[GROUP + part * PACK : GROUP + (part + 1) * PACK, cols].astype(bf16)
                        top = (2 * k + b) * GROUP + part * PACK
                        right[top : top + PACK, tile_cols(j, 0)] = d_re * t_re - d_im * t_im
                        right[top : top + PACK, tile_cols(j, 1)] = d_re * t_im + d_im * t_re
        one = jnp.dot(right[: 2 * batch_size * GROUP], first_ref[...], preferred_element_type=f32).astype(bf16)
        stacks = []
        for k in range(batch_size):
            rows = slice(2 * k * GROUP, (2 * k + 2) * GROUP)
            stacks.append(jnp.concatenate([one[rows, :LANES], one[rows, LANES:]], axis=0))
        exit_waves = jnp.dot(ymat_ref[...], jnp.concatenate(stacks, axis=1), preferred_element_type=f32)
        exit_waves = exit_waves.astype(bf16).astype(f32)
        for k in range(batch_size):
            cols = slice(k * LANES, (k + 1) * LANES)
            re, im = exit_waves[:GROUP, cols], exit_waves[GROUP:, cols]
            slot = slot_list[jnp.minimum(batch_size * batch + k, total - 1)]
            result[slot] = ((re * re + im * im) * (1.0 / beams)).astype(bf16)

    def step(batch, carry):
        rest(batch - 1)
        waves(batch)
        codes_old[...] = codes_new[...]
        return carry

    batches = (total + batch_size - 1) // batch_size
    waves(0)
    codes_old[...] = codes_new[...]
    lax.fori_loop(1, batches, step, 0)
    rest(batches - 1)


def ext_kernel(beams, batch_size, place_ref, near_ref, words_in, mine_ref, other_ref, *refs):
    constants, (low_ref, high_ref, words), out_ref, scratch = refs[:5], refs[5:8], refs[8], refs[9:]
    row_list, col_list, slot_list = scratch[5:]
    side, core, near_base = place_ref[0], place_ref[1], place_ref[3]
    merge_rows(side, core, (mine_ref, other_ref), words_in, words)

    def add(k, found):
        probe = CORES * k + core
        row = near_ref[0, probe] - near_base
        reaches = jnp.where(side == 0, row > -GROUP, row < 4 * GROUP)
        row_list[found] = row
        col_list[found] = near_ref[1, probe]
        slot_list[found] = k
        return found + reaches.astype(jnp.int32)

    total = lax.fori_loop(0, out_ref.shape[0], add, 0, unroll=True)

    few = 6

    @pl.when((total > 0) & (total <= few))
    def _():
        run_tasks(beams, few, side, total, words, *constants, out_ref, scratch)

    @pl.when(total > few)
    def _():
        run_tasks(beams, batch_size, side, total, words, *constants, out_ref, scratch)

    half = low_ref.shape[0]
    low_ref[...] = out_ref[:half]
    high_ref[...] = out_ref[half:]


def own_kernel(beams, batch_size, place_ref, pos_ref, words, *refs):
    constants, (low_ref, high_ref), out_ref, scratch = refs[:5], refs[5:7], refs[7], refs[8:]
    row_list, col_list, slot_list = scratch[5:]
    side, core, row_base = place_ref[0], place_ref[1], place_ref[2]
    count = out_ref.shape[0]

    def add(k, carry):
        probe = CORES * k + core
        row_list[k] = pos_ref[0, probe] - row_base
        col_list[k] = pos_ref[1, probe]
        slot_list[k] = k
        return carry

    lax.fori_loop(0, count, add, 0, unroll=True)
    run_tasks(beams, batch_size, side, count, words, *constants, out_ref, scratch)
    low_ref[...] = out_ref[: count // 2]
    high_ref[...] = out_ref[count // 2 :]


def propagate(beams, place, probes, words, halo, constants):
    count = probes.shape[1] // CORES
    smem = pl.BlockSpec(memory_space=pltpu.SMEM)
    vmem = pl.BlockSpec(memory_space=pltpu.VMEM)
    ext = bool(halo)
    body = ext_kernel if ext else own_kernel
    batch_size = 10 if ext else count

    def kernel(*refs):
        body(beams, batch_size, *refs)

    half = jax.ShapeDtypeStruct((count // 2, GROUP, WIN), jnp.bfloat16)
    return pl.pallas_call(
        kernel,
        out_shape=[half, half, pltpu.VMEM(words.shape, jnp.int32)] if ext else [half, half],
        in_specs=[smem] * 2 + [vmem] * (8 if ext else 6),
        out_specs=[vmem] * (3 if ext else 2),
        input_output_aliases={2: 2} if ext else {},
        scratch_shapes=[
            pltpu.VMEM((count, GROUP, WIN), jnp.bfloat16),
            pltpu.VMEM((batch_size * 3 * GROUP, 4 * LANES), jnp.bfloat16),
            pltpu.VMEM((batch_size, 2, 3 * GROUP, 2 * LANES), jnp.bfloat16),
            pltpu.VMEM((batch_size * 2 * GROUP, 4 * LANES), jnp.bfloat16),
            pltpu.VMEM((batch_size, 2, 2, PACK, LANES), jnp.int16),
            pltpu.VMEM((batch_size, 2, 2, PACK, LANES), jnp.int16),
            pltpu.SMEM((count + 1,), jnp.int32),
            pltpu.SMEM((count + 1,), jnp.int32),
            pltpu.SMEM((count + 1,), jnp.int32),
        ],
        compiler_params=pltpu.CompilerParams(vmem_limit_bytes=40 * MIB),
        cost_estimate=pl.CostEstimate(flops=4 * 10**9, bytes_accessed=4 * 10**6, transcendentals=0),
    )(place, probes, words, *halo, *constants)


def merge_kernel(half, place_ref, pos_ref, own_ref, same_ref, out_ref):
    side, core, row_base = place_ref[0], place_ref[1], place_ref[2]
    line = lax.broadcasted_iota(jnp.int32, (GROUP, LANES), 0).astype(jnp.int16)
    for k in range(out_ref.shape[0]):
        row = pos_ref[0, CORES * (k + half * out_ref.shape[0]) + core] - row_base
        low = jnp.where(side == 0, jnp.clip(row - 2 * GROUP, 0, GROUP), 0)
        high = jnp.where(side == 0, GROUP, jnp.clip(row, 0, GROUP))
        kept = (line >= low.astype(jnp.int16)) & (line < high.astype(jnp.int16))
        out_ref[k] = jnp.where(kept, own_ref[k], same_ref[k])


def merge_pieces(half, place, positions, own, same):
    def kernel(*refs):
        merge_kernel(half, *refs)

    smem = pl.BlockSpec(memory_space=pltpu.SMEM)
    vmem = pl.BlockSpec(memory_space=pltpu.VMEM)
    return pl.pallas_call(
        kernel,
        out_shape=jax.ShapeDtypeStruct(own.shape, own.dtype),
        in_specs=[smem, smem, vmem, vmem],
        out_specs=vmem,
        compiler_params=pltpu.CompilerParams(vmem_limit_bytes=16 * MIB),
    )(place, positions, own, same)


PAD = 3 * WIN + 1


def gather_kernel(place_ref, pos_ref, *refs):
    out_hbm, window, out_buf, sems = refs[8:]
    side, core, row_base = place_ref[0], place_ref[1], place_ref[2]

    def copy(group):
        rows = pl.ds(pl.multiple_of(8 * group, 8), 8)
        return pltpu.make_async_copy(out_buf.at[rows], out_hbm.at[rows], sems.at[group])

    def step(half, local, carry):
        group = local + half * groups // 2
        for par in range(2):
            parity = core if par == 0 else 1 - core
            own, facing = refs[4 * par + half], refs[4 * par + 2 + half]
            for i in range(4):
                row = pos_ref[0, 2 * (4 * group + i) + parity] - row_base
                k = 4 * local + i
                below = row > 2 * GROUP
                start = jnp.where(row < GROUP, row, jnp.where(below, row - GROUP, GROUP))
                base = (2 * i + parity) * PAD + WIN - start
                mine, across = own[k].astype(jnp.float32), facing[k].astype(jnp.float32)
                window[pl.ds(base + GROUP + GROUP * side, GROUP), :] = mine
                window[pl.ds(base + 2 * GROUP - GROUP * side, GROUP), :] = across
                wrapped = jnp.where(below == (side == 0), mine, across)
                window[pl.ds(base + jnp.where(below, 3 * GROUP, 0), GROUP), :] = wrapped
        rows = pl.ds(pl.multiple_of(8 * group, 8), 8)
        for u in range(WIN):
            out_buf[rows, u * WIN : (u + 1) * WIN] = window[pl.ds(WIN + u, 8, stride=PAD), :]
        copy(group).start()
        return carry

    groups = out_buf.shape[0] // 8
    for half in range(2):
        lax.fori_loop(0, groups // 2, lambda local, carry, half=half: step(half, local, carry), 0)
    for group in range(groups):
        copy(group).wait()


def put_together(place, positions, pieces):
    probes = positions.shape[1]
    smem = pl.BlockSpec(memory_space=pltpu.SMEM)
    vmem = pl.BlockSpec(memory_space=pltpu.VMEM)
    return pl.pallas_call(
        gather_kernel,
        out_shape=jax.ShapeDtypeStruct((probes, WIN * WIN), jnp.float32),
        in_specs=[smem, smem] + [vmem] * 8,
        out_specs=pl.BlockSpec(memory_space=pltpu.HBM),
        scratch_shapes=[
            pltpu.VMEM((8 * PAD, LANES), jnp.float32),
            pltpu.VMEM((probes, WIN * WIN), jnp.float32),
            pltpu.SemaphoreType.DMA((probes // 8,)),
        ],
        compiler_params=pltpu.CompilerParams(vmem_limit_bytes=16 * MIB),
    )(place, positions, *pieces)


def local(atoms, phases, aperture, tilts, positions):
    rows_here, width = atoms.shape[1], atoms.shape[2]
    probes = positions.shape[0]
    positions = positions.T
    strip, beam = lax.axis_index("strip"), lax.axis_index("beam")
    strips, ways = lax.axis_size("strip"), lax.axis_size("beam")
    rows_total = rows_here * strips
    beams = tilts.shape[0] * ways
    cores = CORES
    side, core = beam // cores, beam % cores
    near_strip = jnp.where(side == 0, strip - 1 + strips, strip + 1) % strips
    near_base = near_strip * rows_here + jnp.where(side == 0, rows_here, -rows_here)
    place = jnp.stack([side, core, strip * rows_here, near_base]).astype(jnp.int32)

    def across(array, dest):
        pairs = []
        for s in range(strips):
            for b in range(ways):
                to_s, to_b = dest(s, b // cores, b % cores)
                pairs.append((b * strips + s, (to_b[0] * cores + to_b[1]) * strips + to_s % strips))
        return lax.ppermute(array, ("beam", "strip"), pairs)

    def swap_cores(array):
        return across(array, lambda s, y, c: (s, (y, 1 - c)))

    packed = pack_rows(atoms, positions)
    mine = across(packed, lambda s, y, c: (s + 1 - 2 * y, (y, c)))
    packed, tilts, aperture = lax.optimization_barrier((packed, tilts, aperture))
    beam_rows = jnp.concatenate([tilts.astype(jnp.float32), aperture[:, None]], axis=1)
    beam_rows = [
        beam_rows,
        swap_cores(beam_rows),
        across(beam_rows, lambda s, y, c: (s, (1 - y, c))),
        across(beam_rows, lambda s, y, c: (s, (1 - y, 1 - c))),
    ]
    beam_rows = jnp.concatenate(beam_rows, axis=0)
    words = own_words(place, atoms)
    table = probe_table(beam_rows, phases, rows_total, width)
    mine, words, table = lax.optimization_barrier((mine, words, table))
    near = mine[width // cores // LANES * HALO :][:2, :probes].astype(jnp.int32)
    *ext, words = propagate(beams, place, near, words, [mine, swap_cores(mine)], table)
    same = [across(half, lambda s, y, c: (s - 1 + 2 * y, (y, c))) for half in ext]
    own = propagate(beams, place, positions, words, [], table)
    own = [merge_pieces(n, place, positions, *pair) for n, pair in enumerate(zip(own, same))]
    facing = [across(half, lambda s, y, c: (s, (1 - y, c))) for half in own]
    pieces = own + facing
    return put_together(place, positions, pieces + [swap_cores(piece) for piece in pieces])


def solution(mesh):
    in_specs = (P(None, "strip", None), P(), P("beam"), P("beam", None), P("strip", None))
    out_specs = P("strip", None)
    return jax.shard_map(local, mesh=mesh, in_specs=in_specs, out_specs=out_specs, check_vma=False)
```
